32 devices in a mesh: scene: 2 (over y), gx: 4 (over z), gy: 4 (over x, core).
Axes of the slice: x: 2, y: 2, z: 4, core: 2. Of those that a mesh axis runs over, the one named last changes fastest.
Arguments:
- feats: bfloat16 [64, 96, 512], P(('scene', 'gx', 'gy')), parts along dimension 0
- voxel_mask: int32 [64, 512], P(('scene', 'gx', 'gy')), parts along dimension 0, may hold values 0 or 1
- block_slot: int32 [64], P(('scene', 'gx', 'gy')), parts along dimension 0, may hold values from 0 to 3, as said below
- block_count: int32 [32], P(('scene', 'gx', 'gy')), parts along dimension 0, may hold values from 1 to 2, as said below
- weight_one: bfloat16 [96, 2592], replicated, may hold values from -0.125 to 0.125
- weight_two: bfloat16 [96, 2592], replicated, may hold values from -0.125 to 0.125
- gain_one: float32 [96], replicated, may hold values from 0.5 to 1.5
- shift_one: float32 [96], replicated, may hold values from -3 to 3
- gain_two: float32 [96], replicated, may hold values from 0.5 to 1.5
- shift_two: float32 [96], replicated, may hold values from -3 to 3
- cotangent: bfloat16 [64, 96, 512], P(('scene', 'gx', 'gy')), parts along dimension 0, may hold values from -6 to 6
Outputs:
- output: bfloat16 [64, 96, 512], P(('scene', 'gx', 'gy')), parts along dimension 0
- feats_grad: bfloat16 [64, 96, 512], P(('scene', 'gx', 'gy')), parts along dimension 0
- weight_grad_one: float32 [192, 2592], P('scene'), parts along dimension 0
- weight_grad_two: float32 [192, 2592], P('scene'), parts along dimension 0
- norm_grads: float32 [8, 96], P('scene'), parts along dimension 0
The draws below stay inside these ranges and needn't reach their ends.
There are 2 independent parts, one for each index of `scene`. The reference program is written for one: setup_inputs(seed, part) draws one part's arguments, and reference() takes and returns one part's arrays. A program takes and returns all parts, laid end to end along the dimension named above; an argument that names none is the same for every part. Nothing has to cross between parts.
Inputs may be any that keep to these rules, and one draw needn't show every extreme that they name: `block_slot`: the 2 entries of one device name distinct slots of its 4 region slots. `block_count`: some device of every scene has all 2 entries live.
All inputs are finite; a program needn't handle non-finite values. No bound on the sum of `voxel_mask` on one device may be relied on, other than what follows from the above.
Results may differ from the reference program's by a relative error of at most 0.0061.
Values may be sent and summed in bfloat16 or wider, within the bound.
A program may use at most 64 MiB of HBM per device.

```python
import jax
import jax.numpy as jnp
from jax import lax

C = 96
NB = 2
ZB = 1
NBLK = 32
N_GX = 4
N_GY = 4


def draw_feats(key, part):
    key = jax.random.fold_in(key, 11)
    first = jax.random.fold_in(key, 0)
    ramp = jnp.exp(jnp.log(3.0) * jnp.arange(NBLK, dtype=jnp.float32) / NBLK)
    values = jnp.clip(jax.random.normal(first, (NBLK, C, 512), jnp.float32), -6.0, 6.0)
    return (values * ramp[:, None, None]).astype(jnp.bfloat16)


def draw_block_slot(key, part):
    key = jax.random.fold_in(key, 23)
    keys = jax.random.split(key, NBLK // NB)
    orders = jax.vmap(lambda single: jax.random.permutation(single, 2 * NB))(keys)
    return orders[:, :NB].reshape(NBLK).astype(jnp.int32)


def draw_block_count(key, part):
    key = jax.random.fold_in(key, 37)
    first, second = jax.random.split(key)
    devices = NBLK // NB
    counts = jax.random.randint(first, (devices,), 1, NB + 1)
    fullest = jax.random.randint(second, (), 0, devices)
    return jnp.where(jnp.arange(devices) == fullest, NB, counts).astype(jnp.int32)


def set_ends(entries, stream_key, low, top_value):
    index_at = [jax.random.randint(jax.random.fold_in(stream_key, axis), (), 0, length) for axis, length in enumerate(entries.shape)]
    widest = entries.shape.index(max(entries.shape))
    neighbour = index_at[:widest] + [(index_at[widest] + 1) % entries.shape[widest]] + index_at[widest + 1:]
    return entries.at[tuple(index_at)].set(low).at[tuple(neighbour)].set(top_value)


def steps_of(key, shape, cuts, low, largest):
    level = 1.0
    for axis_at, blocks in cuts:
        draws = jax.random.uniform(jax.random.fold_in(jax.random.fold_in(key, 6), axis_at), (blocks,), jnp.float32, low / len(cuts), largest / len(cuts))
        level = level * jnp.repeat(jnp.exp(draws), shape[axis_at] // blocks).reshape((-1,) + (1,) * (len(shape) - 1 - axis_at))
    return level


def scatter_about(own_key, shape, scale, bound, cuts=(), kind=jnp.bfloat16):
    loudness = steps_of(own_key, shape, cuts, -0.22, 0.18) if cuts else 1.0
    values = jax.random.normal(own_key, shape, jnp.float32) * scale * loudness
    return jnp.minimum(jnp.maximum(values, -bound), bound).astype(kind)


def setup_inputs(seed: int = 0, part: int = 0) -> dict:
    streams_of = jax.random.split(jax.random.key(seed), 12)
    own_keys = jax.random.split(jax.random.fold_in(streams_of[11], part), 12)
    feats = draw_feats(jax.random.fold_in(jax.random.fold_in(streams_of[11], part), 71), part)
    voxel_mask = set_ends((jax.random.randint(own_keys[1], (NBLK, 512), 0, 5) < 3).astype(jnp.int32), jax.random.fold_in(own_keys[1], 1), 0, 1)
    block_slot = draw_block_slot(jax.random.fold_in(jax.random.fold_in(streams_of[11], part), 71), part)
    block_count = draw_block_count(jax.random.fold_in(jax.random.fold_in(streams_of[11], part), 71), part)
    weight_one = scatter_about(streams_of[4], (C, 27 * C), (27 * C) ** -0.5, 0.125)
    weight_two = scatter_about(streams_of[5], (C, 27 * C), (27 * C) ** -0.5, 0.125)
    gain_one = jnp.clip(jax.random.uniform(streams_of[6], (C,), jnp.float32, 0.5, 1.5), 0.5, 1.5)
    shift_one = scatter_about(streams_of[7], (C,), 0.5, 3.0, (), jnp.float32)
    gain_two = jnp.clip(jax.random.uniform(streams_of[8], (C,), jnp.float32, 0.5, 1.5), 0.5, 1.5)
    shift_two = scatter_about(streams_of[9], (C,), 0.5, 3.0, (), jnp.float32)
    cotangent = scatter_about(own_keys[10], (NBLK, C, 512), 1.0, 6.0, ((0, 16),))
    return {"feats": feats, "voxel_mask": voxel_mask, "block_slot": block_slot, "block_count": block_count, "weight_one": weight_one, "weight_two": weight_two, "gain_one": gain_one, "shift_one": shift_one, "gain_two": gain_two, "shift_two": shift_two, "cotangent": cotangent}


EPS = 1e-05

def unfold(window):
    channels = window.shape[0]
    pieces = []
    for step_x in range(3):
        for step_y in range(3):
            for step_z in range(3):
                pieces.append(window[:, step_x:step_x + 8, step_y:step_y + 8, step_z:step_z + 8].reshape(channels, 512))
    return jnp.concatenate(pieces, axis=0)

def flipped(weight):
    channels = weight.shape[0]
    return jnp.flip(weight.reshape(channels, 27, channels), axis=1).transpose(2, 1, 0).reshape(channels, 27 * channels)

def silu_slope(values):
    sigma = jax.nn.sigmoid(values)
    return sigma * (1.0 + values * (1.0 - sigma))

def block_places(block_slot):
    index = jnp.arange(NBLK, dtype=jnp.int32)
    device = index // NB
    place_x = device // N_GY * 2 + block_slot // (2 * ZB)
    place_y = device % N_GY * 2 + block_slot // ZB % 2
    place_z = block_slot % ZB
    return jnp.stack([place_x, place_y, place_z], axis=1).astype(jnp.int32)

def scene_grid(blocks, corners):
    channels = blocks.shape[1]
    holder = jnp.zeros((2 * N_GX, 2 * N_GY, ZB, channels, 512), blocks.dtype)
    holder = holder.at[corners[:, 0], corners[:, 1], corners[:, 2]].add(blocks)
    holder = holder.reshape(2 * N_GX, 2 * N_GY, ZB, channels, 8, 8, 8).transpose(3, 0, 4, 1, 5, 2, 6)
    grid = holder.reshape(channels, 16 * N_GX, 16 * N_GY, 8 * ZB)
    return jnp.pad(grid, ((0, 0), (1, 1), (1, 1), (1, 1)))

def window_at(padded, corner):
    channels = padded.shape[0]
    start = (jnp.zeros((), jnp.int32), corner[0] * 8, corner[1] * 8, corner[2] * 8)
    return unfold(lax.dynamic_slice(padded, start, (channels, 10, 10, 10)))

def convolve(blocks, weight, corners):
    padded = scene_grid(blocks, corners)

    def one_block(corner):
        return jnp.dot(weight, window_at(padded, corner), preferred_element_type=jnp.float32)
    return lax.map(one_block, corners)

def weight_grad(blocks, grads, corners):
    padded = scene_grid(blocks, corners)
    channels = blocks.shape[1]

    def add_block(total, item):
        corner, grad = item
        columns = window_at(padded, corner)
        return (total + jnp.dot(grad, columns.T, preferred_element_type=jnp.float32), None)
    total, _ = lax.scan(add_block, jnp.zeros((channels, 27 * channels), jnp.float32), (corners, grads))
    return total

def batch_norm(values, mask, gain, shift):
    count = jnp.sum(mask)
    mean = lax.optimization_barrier(jnp.sum(values, axis=(0, 2))) / count
    centred = (values - mean[None, :, None]) * mask[:, None, :]
    var = lax.optimization_barrier(jnp.sum(centred * centred, axis=(0, 2))) / count
    inv_std = lax.rsqrt(var + EPS)
    normed = centred * inv_std[None, :, None]
    return (normed, normed * gain[None, :, None] + shift[None, :, None], inv_std, count)

def norm_back(grad_z, normed, gain, inv_std, mask, count):
    shift_grad = lax.optimization_barrier(jnp.sum(grad_z, axis=(0, 2)))
    gain_grad = lax.optimization_barrier(jnp.sum(grad_z * normed, axis=(0, 2)))
    scaled = (gain * inv_std)[None, :, None]
    grad = mask[:, None, :] * scaled * (grad_z - shift_grad[None, :, None] / count - normed * gain_grad[None, :, None] / count)
    return (grad.astype(jnp.bfloat16), gain_grad, shift_grad)

def reference(feats, voxel_mask, block_slot, block_count, weight_one, weight_two, gain_one, shift_one, gain_two, shift_two, cotangent):
    corners = block_places(block_slot)
    index = jnp.arange(NBLK, dtype=jnp.int32)
    valid = index % NB < block_count[index // NB]
    mask = voxel_mask.astype(jnp.float32) * valid.astype(jnp.float32)[:, None]
    inputs = feats * mask[:, None, :].astype(jnp.bfloat16)
    conv_one = convolve(inputs, weight_one, corners) * mask[:, None, :]
    normed_one, shifted_one, inv_one, count = batch_norm(conv_one, mask, gain_one, shift_one)
    active = (jax.nn.silu(shifted_one) * mask[:, None, :]).astype(jnp.bfloat16)
    conv_two = convolve(active, weight_two, corners) * mask[:, None, :]
    normed_two, shifted_two, inv_two, count = batch_norm(conv_two, mask, gain_two, shift_two)
    output = (jax.nn.silu(shifted_two) * mask[:, None, :]).astype(jnp.bfloat16)
    grad_z2 = cotangent.astype(jnp.float32) * mask[:, None, :] * silu_slope(shifted_two)
    grad_y2, gain_grad_two, shift_grad_two = norm_back(grad_z2, normed_two, gain_two, inv_two, mask, count)
    weight_grad_two = weight_grad(active, grad_y2, corners)
    grad_a1 = convolve(grad_y2, flipped(weight_two), corners)
    grad_z1 = grad_a1 * mask[:, None, :] * silu_slope(shifted_one)
    grad_y1, gain_grad_one, shift_grad_one = norm_back(grad_z1, normed_one, gain_one, inv_one, mask, count)
    weight_grad_one = weight_grad(inputs, grad_y1, corners)
    feats_grad = (convolve(grad_y1, flipped(weight_one), corners) * mask[:, None, :]).astype(jnp.bfloat16)
    norm_grads = jnp.stack([gain_grad_one, shift_grad_one, gain_grad_two, shift_grad_two])
    return (output, feats_grad, weight_grad_one, weight_grad_two, norm_grads)
```

```python
import functools

import jax
import jax.numpy as jnp
from jax import lax
from jax.experimental import pallas as pl
from jax.experimental.pallas import tpu as pltpu
from jax.sharding import PartitionSpec as P

EPS = 1e-05
F32, BF16 = jnp.float32, jnp.bfloat16
MESH = pl.DeviceIdType.MESH
C = 96
PLANES = 16
SIDES = ((1, 0), (-1, 0), (0, 1), (0, -1), (1, 1), (1, -1), (-1, 1), (-1, -1))
COLS = 27 * C
GROWS = 2048


def silu_slope(values):
    sigma = jax.nn.sigmoid(values)
    return sigma * (1.0 + values * (1.0 - sigma))


def lanes(rows=C):
    return lax.broadcasted_iota(jnp.int32, (rows, 128), 1)


def roll(tile, shift):
    return pltpu.roll(tile, shift, 1)


def kernel(nx, ny, slot_ref, count_ref, mask_ref, params_ref, feats_ref, cot_ref, w1_ref, w2_ref,
           f1_ref, f2_ref,
           out_ref, fg_ref, wg1_ref, wg2_ref, ng_ref,
           rmask, field, cot, val1, val2, tmp, flat, xa, xb, xc, halo, packs, stat_src, stats,
           grad, parts, share, full,
           halo_send, halo_recv, stat_send, stat_recv, rs_send, rs_recv, ag_send, ag_recv):
    group = nx * ny
    gx, gy = lax.axis_index("gx"), lax.axis_index("gy")
    me = gx * ny + gy
    chunk = GROWS // group

    def ident(peer):
        return {"gx": peer // ny, "gy": lax.rem(peer, ny)}

    def each_peer(body):
        def step(j, carry):
            body(j, lax.rem(me + j, group))
            return carry
        lax.fori_loop(1, group, step, 0)

    barrier = pltpu.get_barrier_semaphore()
    each_peer(lambda j, peer: pl.semaphore_signal(
        barrier, inc=1, device_id=ident(peer), device_id_type=MESH))

    live = [(k < count_ref[0]).astype(F32) for k in range(2)]
    hot = [[(slot_ref[k] == s).astype(F32) for s in range(4)] for k in range(2)]

    def place(tile_of, rows, store):
        low = lanes(rows) < 64
        for t in range(4):
            tiles = [tile_of(k, t) for k in range(2)]
            turned = [roll(x, 64) for x in tiles]
            for sx in range(2):
                first = sum(jnp.where(low, hot[k][2 * sx] * tiles[k], hot[k][2 * sx + 1] * turned[k])
                            for k in range(2))
                second = sum(jnp.where(low, hot[k][2 * sx] * turned[k], hot[k][2 * sx + 1] * tiles[k])
                             for k in range(2))
                store(sx * 8 + 2 * t, first)
                store(sx * 8 + 2 * t + 1, second)

    def take(src, ref):
        low = lanes() < 64
        for t in range(4):
            acc = [jnp.zeros((C, 128), F32) for _ in range(2)]
            for sx in range(2):
                a, b = src[sx * 8 + 2 * t], src[sx * 8 + 2 * t + 1]
                left = jnp.where(low, a, roll(b, 64))
                right = jnp.where(low, roll(a, 64), b)
                for k in range(2):
                    acc[k] = acc[k] + hot[k][2 * sx] * left + hot[k][2 * sx + 1] * right
            for k in range(2):
                ref[k, :, t * 128:(t + 1) * 128] = acc[k].astype(BF16)

    def store_mask(p, value):
        rmask[p] = value

    def store_input(p, value):
        field[0, p] = (value * rmask[p][0:1]).astype(BF16)

    def store_cot(p, value):
        cot[p] = (value * rmask[p][0:1]).astype(BF16)

    place(lambda k, t: jnp.broadcast_to(
        mask_ref[k:k + 1, t * 128:(t + 1) * 128].astype(F32) * live[k], (8, 128)), 8, store_mask)
    place(lambda k, t: feats_ref[k, :, t * 128:(t + 1) * 128].astype(F32), C, store_input)

    def halo_copy(ex, d, src):
        dx, dy = SIDES[d]
        return pltpu.make_async_remote_copy(
            src_ref=src, dst_ref=halo.at[ex, d],
            send_sem=halo_send.at[ex, d], recv_sem=halo_recv.at[ex, d],
            device_id={"gx": gx + dx, "gy": gy + dy}, device_id_type=MESH)

    def inside(dx, dy):
        return (gx + dx >= 0) & (gx + dx < nx) & (gy + dy >= 0) & (gy + dy < ny)

    def halo_sources(ex):
        srcs = []
        for d, (dx, dy) in enumerate(SIDES):
            if dx == 0:
                srcs.append(packs.at[ex, 0 if dy == 1 else 1])
            else:
                srcs.append(field.at[ex, PLANES - 1 if dx == 1 else 0])
        return srcs

    for d, (dx, dy) in enumerate(SIDES):
        @pl.when(jnp.logical_not(inside(-dx, -dy)))
        def _(d=d):
            for ex in range(4):
                halo[ex, d] = jnp.zeros((C, 128), BF16)

    def send_halo(ex):
        lane = lanes()

        def pack(i, carry):
            high, low = carry
            plane = field[ex, i].astype(F32)
            here = (lane >= i * 8) & (lane < i * 8 + 8)
            high = jnp.where(here, roll(plane, lax.rem(i * 8 + 8, 128)), high)
            low = jnp.where(here, roll(plane, i * 8), low)
            return high, low

        zero = jnp.zeros((C, 128), F32)
        high, low = lax.fori_loop(0, PLANES, pack, (zero, zero))
        packs[ex, 0] = high.astype(BF16)
        packs[ex, 1] = low.astype(BF16)
        srcs = halo_sources(ex)
        for d, (dx, dy) in enumerate(SIDES):
            @pl.when(inside(dx, dy))
            def _(d=d):
                halo_copy(ex, d, srcs[d]).start()

    def wait_halo(ex):
        srcs = halo_sources(ex)
        for d, (dx, dy) in enumerate(SIDES):
            @pl.when(inside(-dx, -dy))
            def _(d=d):
                halo_copy(ex, d, srcs[d]).wait_recv()

    def done_halo(ex):
        srcs = halo_sources(ex)
        for d, (dx, dy) in enumerate(SIDES):
            @pl.when(inside(dx, dy))
            def _(d=d):
                halo_copy(ex, d, srcs[d]).wait_send()

    def side(ex, dx, dy):
        return halo[ex, SIDES.index((-dx, -dy))].astype(F32)

    def spread(x, p, plane, edge):
        lane = lanes()
        z = lane % 8
        for oy in (-1, 0, 1):
            src = plane
            if oy == 1:
                src = jnp.where(lane < 8, edge, plane)
            elif oy == -1:
                src = jnp.where(lane >= 120, edge, plane)
            for oz in (-1, 0, 1):
                shift = (-(8 * oy + oz)) % 128
                r = roll(src, shift) if shift else src
                if oz == 1:
                    r = jnp.where(z < 7, r, 0.0)
                elif oz == -1:
                    r = jnp.where(z > 0, r, 0.0)
                row = ((oy + 1) * 3 + oz + 1) * C
                start = p * 128 if isinstance(p, int) else pl.multiple_of(p * 128, 128)
                x[row:row + C, pl.ds(start, 128)] = r.astype(BF16)

    def unfold(ex, x):
        lane = lanes()
        for p, dx in ((0, -1), (PLANES + 1, 1)):
            edge = jnp.where(lane < 64, side(ex, dx, 1), side(ex, dx, -1))
            spread(x, p, side(ex, dx, 0), edge)

        def body(i, carry):
            before = roll(side(ex, 0, -1), lax.rem(248 - i * 8, 128))
            after = roll(side(ex, 0, 1), lax.rem(128 - i * 8, 128))
            spread(x, i + 1, field[ex, i].astype(F32), jnp.where(lane < 64, after, before))
            return carry
        lax.fori_loop(0, PLANES, body, 0)

    def conv(w_ref, x, store):
        def body(j, carry):
            acc = None
            for ox in range(3):
                cols = x[:, pl.ds(pl.multiple_of((2 * j + ox) * 128, 128), 256)]
                part = jnp.dot(w_ref[ox], cols, preferred_element_type=F32)
                acc = part if acc is None else acc + part
            for h in range(2):
                carry = store(2 * j + h, acc[:, h * 128:(h + 1) * 128], carry)
            return carry
        return body

    def run_conv(w_ref, x, store, init):
        return lax.fori_loop(0, PLANES // 2, conv(w_ref, x, store), init)

    def pack_columns(columns):
        lane = lanes(C)
        tile = jnp.zeros((C, 128), F32)
        for i, column in enumerate(columns):
            tile = jnp.where(lane == i, column, tile)
        whole = jnp.concatenate([tile, jnp.zeros((128 - C, 128), F32)], axis=0)
        return jnp.transpose(whole)[0:8]

    def to_columns(rows):
        whole = jnp.concatenate(rows + [jnp.zeros((128 - len(rows), 128), F32)], axis=0)
        turned = jnp.transpose(whole)
        return [turned[0:C, i:i + 1] for i in range(len(rows))]

    def stat_copy(ph, j, peer, slot):
        return pltpu.make_async_remote_copy(
            src_ref=stat_src.at[ph], dst_ref=stats.at[ph, slot],
            send_sem=stat_send.at[ph, j], recv_sem=stat_recv.at[ph, slot],
            device_id=ident(peer), device_id_type=MESH)

    def send_stats(ph, tile):
        stat_src[ph] = tile
        stats[ph, me] = tile
        each_peer(lambda j, peer: stat_copy(ph, j, peer, me).start())

    def wait_stats(ph):
        each_peer(lambda j, peer: stat_copy(ph, j, peer, peer).wait_recv())

    def done_stats(ph):
        each_peer(lambda j, peer: stat_copy(ph, j, peer, me).wait_send())

    def total_stats(ph):
        return lax.fori_loop(0, group, lambda i, acc: acc + stats[ph, i], jnp.zeros((8, 128), F32))

    def total(tile):
        return jnp.sum(tile, axis=1, keepdims=True)

    zero_tile = jnp.zeros((C, 128), F32)
    here = lax.fori_loop(0, PLANES, lambda i, acc: acc + rmask[i], jnp.zeros((8, 128), F32))
    here = jnp.sum(here[0:1], axis=1, keepdims=True)

    def moments(ph, val, summed):
        mean = total(summed) / jnp.maximum(here, 1.0)

        def body(i, acc):
            centred = (val[i] - mean) * rmask[i][0:1]
            return acc + centred * centred
        spread_sum = total(lax.fori_loop(0, PLANES, body, zero_tile))
        send_stats(ph, pack_columns([total(summed), spread_sum, jnp.broadcast_to(here, (C, 1))]))
        wait_stats(ph)
        sums = total_stats(ph)
        count = jnp.maximum(jnp.max(sums[2:3], axis=1, keepdims=True), 1.0)
        mean_row = sums[0:1] / count

        def shifted(i, acc):
            tile = stats[ph, i]
            n = tile[2:3]
            gap = tile[0:1] / jnp.maximum(n, 1.0) - mean_row
            return acc + tile[1:2] + n * gap * gap
        square = lax.fori_loop(0, group, shifted, jnp.zeros((1, 128), F32))
        inv_row = lax.rsqrt(square / count + EPS)
        mean_col, inv_col = to_columns([mean_row, inv_row])
        return mean_col, inv_col, 1.0 / count

    def store_conv(val):
        def store(p, tile, acc):
            y = tile * rmask[p][0:1]
            val[p] = y
            return acc + y
        return store

    gain1, shift1, gain2, shift2 = to_columns([params_ref[i:i + 1] for i in range(4)])

    pl.semaphore_wait(barrier, group - 1)
    send_halo(0)
    place(lambda k, t: cot_ref[k, :, t * 128:(t + 1) * 128].astype(F32), C, store_cot)
    wait_halo(0)
    unfold(0, xa)
    summed = run_conv(w1_ref, xa, store_conv(val1), zero_tile)
    mean1, inv1, per = moments(0, val1, summed)

    def act_one(i, carry):
        m = rmask[i][0:1]
        normed = (val1[i] - mean1) * m * inv1
        val1[i] = normed
        z = normed * gain1 + shift1
        field[1, i] = (z * jax.nn.sigmoid(z) * m).astype(BF16)
        return carry
    lax.fori_loop(0, PLANES, act_one, 0)

    send_halo(1)
    wait_halo(1)
    unfold(1, xb)
    summed = run_conv(w2_ref, xb, store_conv(val2), zero_tile)
    mean2, inv2, per = moments(1, val2, summed)

    def act_two(i, carry):
        a, b = carry
        m = rmask[i][0:1]
        normed = (val2[i] - mean2) * m * inv2
        val2[i] = normed
        z = normed * gain2 + shift2
        sigma = jax.nn.sigmoid(z)
        tmp[0, i] = z * sigma * m
        gz = cot[i].astype(F32) * (sigma * (1.0 + z * (1.0 - sigma)))
        tmp[1, i] = gz
        return a + gz, b + gz * normed
    sg, gg = lax.fori_loop(0, PLANES, act_two, (zero_tile, zero_tile))

    def send_back(ph, sg, gg):
        send_stats(ph, pack_columns([total(sg), total(gg)]))

    def finish_back(ph, row):
        wait_stats(ph)
        sums = total_stats(ph)
        ng_ref[row:row + 1, :] = sums[1:2, 0:C]
        ng_ref[row + 1:row + 2, :] = sums[0:1, 0:C]
        return to_columns([sums[0:1], sums[1:2]])

    def back(ex, val, gz_slot, gain, inv, sums):
        sg, gg = sums[0] * per, sums[1] * per
        scaled = gain * inv

        def body(i, carry):
            g = rmask[i][0:1] * scaled * (tmp[gz_slot, i] - sg - val[i] * gg)
            g = g.astype(BF16)
            field[ex, i] = g
            flat[:, pl.ds(pl.multiple_of(i * 128, 128), 128)] = g
            return carry
        lax.fori_loop(0, PLANES, body, 0)

    send_back(2, sg, gg)
    take(tmp.at[0], out_ref)
    back(2, val2, 1, gain2, inv2, finish_back(2, 2))
    send_halo(2)

    def kernel_grad(w, x):
        for b in range((COLS + 255) // 256):
            lo, hi = b * 256, min(b * 256 + 256, COLS)
            pieces = []
            for ox in range(3):
                first, last = max(lo, ox * 9 * C), min(hi, (ox + 1) * 9 * C)
                if first < last:
                    pieces.append(x[first - ox * 9 * C:last - ox * 9 * C,
                                    ox * 128:ox * 128 + PLANES * 128])
            rhs = pieces[0] if len(pieces) == 1 else jnp.concatenate(pieces, axis=0)
            part = lax.dot_general(flat[...], rhs, (((1,), (1,)), ((), ())),
                                   preferred_element_type=F32).astype(BF16)
            for h in range(0, hi - lo, 128):
                tile = part[:, h:min(h + 128, hi - lo)]
                if tile.shape[1] < 128:
                    tile = jnp.concatenate(
                        [tile, jnp.zeros((C, 128 - tile.shape[1]), BF16)], axis=1)
                row = (lo + h) // 128 * C
                grad[w, row:row + C] = tile
        grad[w, 21 * C:GROWS] = jnp.zeros((GROWS - 21 * C, 128), BF16)

    def rows_of(i):
        return pl.ds(pl.multiple_of(i * chunk, chunk), chunk)

    def rs_copy(w, j, peer, slot):
        return pltpu.make_async_remote_copy(
            src_ref=grad.at[w, rows_of(peer)], dst_ref=parts.at[w, slot],
            send_sem=rs_send.at[w, j], recv_sem=rs_recv.at[w, slot],
            device_id=ident(peer), device_id_type=MESH)

    def ag_copy(w, j, peer, slot):
        return pltpu.make_async_remote_copy(
            src_ref=share.at[w], dst_ref=full.at[w, rows_of(slot)],
            send_sem=ag_send.at[w, j], recv_sem=ag_recv.at[w, slot],
            device_id=ident(peer), device_id_type=MESH)

    def start_rs(w):
        parts[w, me] = grad[w, rows_of(me)]
        each_peer(lambda j, peer: rs_copy(w, j, peer, me).start())

    def finish_rs(w):
        each_peer(lambda j, peer: rs_copy(w, j, peer, peer).wait_recv())
        summed = lax.fori_loop(0, group, lambda i, acc: acc + parts[w, i].astype(F32),
                               jnp.zeros((chunk, 128), F32)).astype(BF16)
        share[w] = summed
        full[w, rows_of(me)] = summed
        each_peer(lambda j, peer: ag_copy(w, j, peer, me).start())

    def finish_ag(w, ref):
        each_peer(lambda j, peer: ag_copy(w, j, peer, peer).wait_recv())
        for t in range(21):
            wide = min(128, COLS - t * 128)
            ref[:, t * 128:t * 128 + wide] = full[w, t * C:(t + 1) * C].astype(F32)[:, 0:wide]

    kernel_grad(1, xb)
    start_rs(1)
    wait_halo(2)
    unfold(2, xc)

    def store_gz(p, tile, carry):
        a, b = carry
        normed = val1[p]
        z = normed * gain1 + shift1
        gz = tile * rmask[p][0:1] * silu_slope(z)
        tmp[0, p] = gz
        return a + gz, b + gz * normed
    sg, gg = run_conv(f2_ref, xc, store_gz, (zero_tile, zero_tile))
    send_back(3, sg, gg)
    finish_rs(1)
    back(3, val1, 0, gain1, inv1, finish_back(3, 0))
    send_halo(3)
    kernel_grad(0, xa)
    start_rs(0)
    wait_halo(3)
    unfold(3, xc)

    def store_fg(p, tile, carry):
        tmp[1, p] = tile * rmask[p][0:1]
        return carry
    run_conv(f1_ref, xc, store_fg, 0)
    take(tmp.at[1], fg_ref)
    finish_rs(0)
    finish_ag(1, wg2_ref)
    finish_ag(0, wg1_ref)

    for ex in range(4):
        done_halo(ex)
        done_stats(ex)
    for w in range(2):
        each_peer(lambda j, peer: rs_copy(w, j, peer, me).wait_send())
        each_peer(lambda j, peer: ag_copy(w, j, peer, me).wait_send())


def split(weight):
    return weight.reshape(C, 3, 9 * C).transpose(1, 0, 2)


def flipped(weight):
    return jnp.flip(weight.reshape(C, 3, 9, C), axis=(1, 2)).transpose(1, 3, 2, 0).reshape(3, C, 9 * C)


def per_device(nx, ny, feats, voxel_mask, block_slot, block_count, weight_one, weight_two,
               gain_one, shift_one, gain_two, shift_two, cotangent):
    group = nx * ny
    params = jnp.pad(jnp.stack([gain_one, shift_one, gain_two, shift_two]), ((0, 4), (0, 128 - C)))
    vmem = pl.BlockSpec(memory_space=pltpu.VMEM)
    smem = pl.BlockSpec(memory_space=pltpu.SMEM)
    shapes = [
        jax.ShapeDtypeStruct((2, C, 512), BF16),
        jax.ShapeDtypeStruct((2, C, 512), BF16),
        jax.ShapeDtypeStruct((C, COLS), F32),
        jax.ShapeDtypeStruct((C, COLS), F32),
        jax.ShapeDtypeStruct((4, C), F32),
    ]
    wide = (PLANES + 2) * 128
    dma = pltpu.SemaphoreType.DMA
    return pl.pallas_call(
        functools.partial(kernel, nx, ny),
        out_shape=shapes,
        in_specs=[smem, smem] + [vmem] * 8,
        out_specs=[vmem] * 5,
        scratch_shapes=[
            pltpu.VMEM((PLANES, 8, 128), F32),
            pltpu.VMEM((4, PLANES, C, 128), BF16),
            pltpu.VMEM((PLANES, C, 128), BF16),
            pltpu.VMEM((PLANES, C, 128), F32),
            pltpu.VMEM((PLANES, C, 128), F32),
            pltpu.VMEM((2, PLANES, C, 128), F32),
            pltpu.VMEM((C, PLANES * 128), BF16),
            pltpu.VMEM((9 * C, wide), BF16),
            pltpu.VMEM((9 * C, wide), BF16),
            pltpu.VMEM((9 * C, wide), BF16),
            pltpu.VMEM((4, 8, C, 128), BF16),
            pltpu.VMEM((4, 2, C, 128), BF16),
            pltpu.VMEM((4, 8, 128), F32),
            pltpu.VMEM((4, group, 8, 128), F32),
            pltpu.VMEM((2, GROWS, 128), BF16),
            pltpu.VMEM((2, group, GROWS // group, 128), BF16),
            pltpu.VMEM((2, GROWS // group, 128), BF16),
            pltpu.VMEM((2, GROWS, 128), BF16),
            dma((4, 8)), dma((4, 8)),
            dma((4, group)), dma((4, group)),
            dma((2, group)), dma((2, group)),
            dma((2, group)), dma((2, group)),
        ],
        compiler_params=pltpu.CompilerParams(
            collective_id=0, has_side_effects=True, vmem_limit_bytes=48 * 1024 * 1024),
        name="section",
    )(block_slot, block_count, voxel_mask, params, feats, cotangent,
      split(weight_one), split(weight_two), flipped(weight_one), flipped(weight_two))


def solution(mesh):
    rows = ("scene", "gx", "gy")
    placed = (
        P(rows, None, None), P(rows, None), P(rows), P(rows),
        P(), P(), P(), P(), P(), P(), P(rows, None, None),
    )
    return jax.shard_map(
        functools.partial(per_device, mesh.shape["gx"], mesh.shape["gy"]),
        mesh=mesh,
        in_specs=placed,
        out_specs=(
            P(rows, None, None), P(rows, None, None),
            P("scene", None), P("scene", None), P("scene", None),
        ),
        check_vma=False,
    )
```

```python
import functools

import jax
import jax.numpy as jnp
from jax import lax
from jax.experimental import pallas as pl
from jax.experimental.pallas import tpu as pltpu
from jax.sharding import PartitionSpec as P

EPS = 1e-05
F32, BF16 = jnp.float32, jnp.bfloat16
MESH = pl.DeviceIdType.MESH
C = 96
PLANES = 16
SIDES = ((1, 0), (-1, 0), (0, 1), (0, -1), (1, 1), (1, -1), (-1, 1), (-1, -1))
COLS = 27 * C
GROWS = 2048


def silu_slope(values):
    sigma = jax.nn.sigmoid(values)
    return sigma * (1.0 + values * (1.0 - sigma))


def lanes(rows=C):
    return lax.broadcasted_iota(jnp.int32, (rows, 128), 1)


def roll(tile, shift):
    return pltpu.roll(tile, shift, 1)


def kernel(nx, ny, slot_ref, count_ref, mask_ref, params_ref, feats_ref, cot_ref, w1_ref, w2_ref,
           out_ref, fg_ref, wg1_ref, wg2_ref, ng_ref,
           rmask, field, cot, val1, val2, tmp, flat, xa, xb, xc, turned_w, f1_ref, f2_ref, halo, packs, stat_src, stats,
           grad, parts, share, full,
           halo_send, halo_recv, stat_send, stat_recv, rs_send, rs_recv, ag_send, ag_recv):
    group = nx * ny
    gx, gy = lax.axis_index("gx"), lax.axis_index("gy")
    me = gx * ny + gy
    chunk = GROWS // group

    def ident(peer):
        return {"gx": peer // ny, "gy": lax.rem(peer, ny)}

    def each_peer(body):
        def step(j, carry):
            body(j, lax.rem(me + j, group))
            return carry
        lax.fori_loop(1, group, step, 0)

    barrier = pltpu.get_barrier_semaphore()
    each_peer(lambda j, peer: pl.semaphore_signal(
        barrier, inc=1, device_id=ident(peer), device_id_type=MESH))

    live = [(k < count_ref[0]).astype(F32) for k in range(2)]
    hot = [[(slot_ref[k] == s).astype(F32) for s in range(4)] for k in range(2)]

    def place(tile_of, rows, store):
        low = lanes(rows) < 64
        for t in range(4):
            tiles = [tile_of(k, t) for k in range(2)]
            turned = [roll(x, 64) for x in tiles]
            for sx in range(2):
                first = sum(jnp.where(low, hot[k][2 * sx] * tiles[k], hot[k][2 * sx + 1] * turned[k])
                            for k in range(2))
                second = sum(jnp.where(low, hot[k][2 * sx] * turned[k], hot[k][2 * sx + 1] * tiles[k])
                             for k in range(2))
                store(sx * 8 + 2 * t, first)
                store(sx * 8 + 2 * t + 1, second)

    def take(src, ref):
        low = lanes() < 64
        for t in range(4):
            acc = [jnp.zeros((C, 128), F32) for _ in range(2)]
            for sx in range(2):
                a, b = src[sx * 8 + 2 * t], src[sx * 8 + 2 * t + 1]
                left = jnp.where(low, a, roll(b, 64))
                right = jnp.where(low, roll(a, 64), b)
                for k in range(2):
                    acc[k] = acc[k] + hot[k][2 * sx] * left + hot[k][2 * sx + 1] * right
            for k in range(2):
                ref[k, :, t * 128:(t + 1) * 128] = acc[k].astype(BF16)

    def store_mask(p, value):
        rmask[p] = value

    def store_input(p, value):
        field[0, p] = (value * rmask[p][0:1]).astype(BF16)

    def store_cot(p, value):
        cot[p] = (value * rmask[p][0:1]).astype(BF16)

    place(lambda k, t: jnp.broadcast_to(
        mask_ref[k:k + 1, t * 128:(t + 1) * 128].astype(F32) * live[k], (8, 128)), 8, store_mask)
    place(lambda k, t: feats_ref[k, :, t * 128:(t + 1) * 128].astype(F32), C, store_input)

    def halo_copy(ex, d, src):
        dx, dy = SIDES[d]
        return pltpu.make_async_remote_copy(
            src_ref=src, dst_ref=halo.at[ex, d],
            send_sem=halo_send.at[ex, d], recv_sem=halo_recv.at[ex, d],
            device_id={"gx": gx + dx, "gy": gy + dy}, device_id_type=MESH)

    def inside(dx, dy):
        return (gx + dx >= 0) & (gx + dx < nx) & (gy + dy >= 0) & (gy + dy < ny)

    def halo_sources(ex):
        srcs = []
        for d, (dx, dy) in enumerate(SIDES):
            if dx == 0:
                srcs.append(packs.at[ex, 0 if dy == 1 else 1])
            else:
                srcs.append(field.at[ex, PLANES - 1 if dx == 1 else 0])
        return srcs

    for d, (dx, dy) in enumerate(SIDES):
        @pl.when(jnp.logical_not(inside(-dx, -dy)))
        def _(d=d):
            for ex in range(4):
                halo[ex, d] = jnp.zeros((C, 128), BF16)

    def send_halo(ex):
        lane = lanes()

        def pack(i, carry):
            high, low = carry
            plane = field[ex, i].astype(F32)
            here = (lane >= i * 8) & (lane < i * 8 + 8)
            high = jnp.where(here, roll(plane, lax.rem(i * 8 + 8, 128)), high)
            low = jnp.where(here, roll(plane, i * 8), low)
            return high, low

        zero = jnp.zeros((C, 128), F32)
        high, low = lax.fori_loop(0, PLANES, pack, (zero, zero))
        packs[ex, 0] = high.astype(BF16)
        packs[ex, 1] = low.astype(BF16)
        srcs = halo_sources(ex)
        for d, (dx, dy) in enumerate(SIDES):
            @pl.when(inside(dx, dy))
            def _(d=d):
                halo_copy(ex, d, srcs[d]).start()

    def wait_halo(ex):
        srcs = halo_sources(ex)
        for d, (dx, dy) in enumerate(SIDES):
            @pl.when(inside(-dx, -dy))
            def _(d=d):
                halo_copy(ex, d, srcs[d]).wait_recv()

    def done_halo(ex):
        srcs = halo_sources(ex)
        for d, (dx, dy) in enumerate(SIDES):
            @pl.when(inside(dx, dy))
            def _(d=d):
                halo_copy(ex, d, srcs[d]).wait_send()

    def side(ex, dx, dy):
        return halo[ex, SIDES.index((-dx, -dy))].astype(F32)

    def spread(x, p, plane, edge):
        lane = lanes()
        z = lane % 8
        for oy in (-1, 0, 1):
            src = plane
            if oy == 1:
                src = jnp.where(lane < 8, edge, plane)
            elif oy == -1:
                src = jnp.where(lane >= 120, edge, plane)
            for oz in (-1, 0, 1):
                shift = (-(8 * oy + oz)) % 128
                r = roll(src, shift) if shift else src
                if oz == 1:
                    r = jnp.where(z < 7, r, 0.0)
                elif oz == -1:
                    r = jnp.where(z > 0, r, 0.0)
                row = ((oy + 1) * 3 + oz + 1) * C
                start = p * 128 if isinstance(p, int) else pl.multiple_of(p * 128, 128)
                x[row:row + C, pl.ds(start, 128)] = r.astype(BF16)

    def unfold(ex, x):
        lane = lanes()
        for p, dx in ((0, -1), (PLANES + 1, 1)):
            edge = jnp.where(lane < 64, side(ex, dx, 1), side(ex, dx, -1))
            spread(x, p, side(ex, dx, 0), edge)

        def body(i, carry):
            before = roll(side(ex, 0, -1), lax.rem(248 - i * 8, 128))
            after = roll(side(ex, 0, 1), lax.rem(128 - i * 8, 128))
            spread(x, i + 1, field[ex, i].astype(F32), jnp.where(lane < 64, after, before))
            return carry
        lax.fori_loop(0, PLANES, body, 0)

    def slabs():
        return [(lo, min(lo + 256, COLS)) for lo in range(0, COLS, 256)]

    def pieces_of(lo, hi):
        found = []
        for ox in range(3):
            first, last = max(lo, ox * 9 * C), min(hi, (ox + 1) * 9 * C)
            if first < last:
                found.append((ox, first - ox * 9 * C, last - ox * 9 * C))
        return found

    def joined(pieces):
        return pieces[0] if len(pieces) == 1 else jnp.concatenate(pieces, axis=0)

    def flip(w_ref, out):
        for lo in range(0, COLS, 128):
            wide = min(128, COLS - lo)
            tile = w_ref[:, lo:lo + wide].astype(F32)
            if wide < 128:
                tile = jnp.concatenate([tile, jnp.zeros((C, 128 - wide), F32)], axis=1)
            tile = jnp.concatenate([tile, jnp.zeros((128 - C, 128), F32)], axis=0)
            turned_w[lo:lo + 128] = jnp.transpose(tile)
        lane = lanes()
        for lo in range(0, COLS, 128):
            tile = jnp.zeros((C, 128), F32)
            for o in range(27):
                to = o * C - lo
                if to < 128 and to + C > 0:
                    block = turned_w[(26 - o) * C:(27 - o) * C]
                    block = roll(block, to % 128) if to % 128 else block
                    tile = jnp.where((lane >= to) & (lane < to + C), block, tile)
            out[:, lo:lo + 128] = tile.astype(BF16)

    def conv(w_ref, x, store):
        def body(j, carry):
            acc = None
            for lo, hi in slabs():
                cols = [x[a:b, pl.ds(pl.multiple_of((2 * j + ox) * 128, 128), 256)]
                        for ox, a, b in pieces_of(lo, hi)]
                part = jnp.dot(w_ref[:, lo:hi], joined(cols), preferred_element_type=F32)
                acc = part if acc is None else acc + part
            for h in range(2):
                carry = store(2 * j + h, acc[:, h * 128:(h + 1) * 128], carry)
            return carry
        return body

    def run_conv(w_ref, x, store, init):
        return lax.fori_loop(0, PLANES // 2, conv(w_ref, x, store), init)

    def pack_columns(columns):
        lane = lanes(C)
        tile = jnp.zeros((C, 128), F32)
        for i, column in enumerate(columns):
            tile = jnp.where(lane == i, column, tile)
        whole = jnp.concatenate([tile, jnp.zeros((128 - C, 128), F32)], axis=0)
        return jnp.transpose(whole)[0:8]

    def to_columns(rows):
        whole = jnp.concatenate(rows + [jnp.zeros((128 - len(rows), 128), F32)], axis=0)
        turned = jnp.transpose(whole)
        return [turned[0:C, i:i + 1] for i in range(len(rows))]

    def stat_copy(ph, j, peer, slot):
        return pltpu.make_async_remote_copy(
            src_ref=stat_src.at[ph], dst_ref=stats.at[ph, slot],
            send_sem=stat_send.at[ph, j], recv_sem=stat_recv.at[ph, slot],
            device_id=ident(peer), device_id_type=MESH)

    def send_stats(ph, tile):
        stat_src[ph] = tile
        stats[ph, me] = tile
        each_peer(lambda j, peer: stat_copy(ph, j, peer, me).start())

    def wait_stats(ph):
        each_peer(lambda j, peer: stat_copy(ph, j, peer, peer).wait_recv())

    def done_stats(ph):
        each_peer(lambda j, peer: stat_copy(ph, j, peer, me).wait_send())

    def total_stats(ph):
        return lax.fori_loop(0, group, lambda i, acc: acc + stats[ph, i], jnp.zeros((8, 128), F32))

    def total(tile):
        return jnp.sum(tile, axis=1, keepdims=True)

    zero_tile = jnp.zeros((C, 128), F32)
    here = lax.fori_loop(0, PLANES, lambda i, acc: acc + rmask[i], jnp.zeros((8, 128), F32))
    here = jnp.sum(here[0:1], axis=1, keepdims=True)

    def moments(ph, val, summed):
        mean = total(summed) / jnp.maximum(here, 1.0)

        def body(i, acc):
            centred = (val[i] - mean) * rmask[i][0:1]
            return acc + centred * centred
        spread_sum = total(lax.fori_loop(0, PLANES, body, zero_tile))
        send_stats(ph, pack_columns([total(summed), spread_sum, jnp.broadcast_to(here, (C, 1))]))
        wait_stats(ph)
        sums = total_stats(ph)
        count = jnp.maximum(jnp.max(sums[2:3], axis=1, keepdims=True), 1.0)
        mean_row = sums[0:1] / count

        def shifted(i, acc):
            tile = stats[ph, i]
            n = tile[2:3]
            gap = tile[0:1] / jnp.maximum(n, 1.0) - mean_row
            return acc + tile[1:2] + n * gap * gap
        square = lax.fori_loop(0, group, shifted, jnp.zeros((1, 128), F32))
        inv_row = lax.rsqrt(square / count + EPS)
        mean_col, inv_col = to_columns([mean_row, inv_row])
        return mean_col, inv_col, 1.0 / count

    def store_conv(val):
        def store(p, tile, acc):
            y = tile * rmask[p][0:1]
            val[p] = y
            return acc + y
        return store

    gain1, shift1, gain2, shift2 = to_columns([params_ref[i:i + 1] for i in range(4)])

    pl.semaphore_wait(barrier, group - 1)
    send_halo(0)
    place(lambda k, t: cot_ref[k, :, t * 128:(t + 1) * 128].astype(F32), C, store_cot)
    flip(w2_ref, f2_ref)
    flip(w1_ref, f1_ref)
    wait_halo(0)
    unfold(0, xa)
    summed = run_conv(w1_ref, xa, store_conv(val1), zero_tile)
    mean1, inv1, per = moments(0, val1, summed)

    def act_one(i, carry):
        m = rmask[i][0:1]
        normed = (val1[i] - mean1) * m * inv1
        val1[i] = normed
        z = normed * gain1 + shift1
        field[1, i] = (z * jax.nn.sigmoid(z) * m).astype(BF16)
        return carry
    lax.fori_loop(0, PLANES, act_one, 0)

    send_halo(1)
    wait_halo(1)
    unfold(1, xb)
    summed = run_conv(w2_ref, xb, store_conv(val2), zero_tile)
    mean2, inv2, per = moments(1, val2, summed)

    def act_two(i, carry):
        a, b = carry
        m = rmask[i][0:1]
        normed = (val2[i] - mean2) * m * inv2
        val2[i] = normed
        z = normed * gain2 + shift2
        sigma = jax.nn.sigmoid(z)
        tmp[0, i] = z * sigma * m
        gz = cot[i].astype(F32) * (sigma * (1.0 + z * (1.0 - sigma)))
        tmp[1, i] = gz
        return a + gz, b + gz * normed
    sg, gg = lax.fori_loop(0, PLANES, act_two, (zero_tile, zero_tile))

    def send_back(ph, sg, gg):
        send_stats(ph, pack_columns([total(sg), total(gg)]))

    def finish_back(ph, row):
        wait_stats(ph)
        sums = total_stats(ph)
        ng_ref[row:row + 1, :] = sums[1:2, 0:C]
        ng_ref[row + 1:row + 2, :] = sums[0:1, 0:C]
        return to_columns([sums[0:1], sums[1:2]])

    def back(ex, val, gz_slot, gain, inv, sums):
        sg, gg = sums[0] * per, sums[1] * per
        scaled = gain * inv

        def body(i, carry):
            g = rmask[i][0:1] * scaled * (tmp[gz_slot, i] - sg - val[i] * gg)
            g = g.astype(BF16)
            field[ex, i] = g
            flat[:, pl.ds(pl.multiple_of(i * 128, 128), 128)] = g
            return carry
        lax.fori_loop(0, PLANES, body, 0)

    send_back(2, sg, gg)
    take(tmp.at[0], out_ref)
    back(2, val2, 1, gain2, inv2, finish_back(2, 2))
    send_halo(2)

    def kernel_grad(w, x):
        for lo, hi in slabs():
            rhs = joined([x[a:b, ox * 128:ox * 128 + PLANES * 128]
                          for ox, a, b in pieces_of(lo, hi)])
            part = lax.dot_general(flat[...], rhs, (((1,), (1,)), ((), ())),
                                   preferred_element_type=F32).astype(BF16)
            for h in range(0, hi - lo, 128):
                tile = part[:, h:min(h + 128, hi - lo)]
                if tile.shape[1] < 128:
                    tile = jnp.concatenate(
                        [tile, jnp.zeros((C, 128 - tile.shape[1]), BF16)], axis=1)
                row = (lo + h) // 128 * C
                grad[w, row:row + C] = tile
        grad[w, 21 * C:GROWS] = jnp.zeros((GROWS - 21 * C, 128), BF16)

    def rows_of(i):
        return pl.ds(pl.multiple_of(i * chunk, chunk), chunk)

    def rs_copy(w, j, peer, slot):
        return pltpu.make_async_remote_copy(
            src_ref=grad.at[w, rows_of(peer)], dst_ref=parts.at[w, slot],
            send_sem=rs_send.at[w, j], recv_sem=rs_recv.at[w, slot],
            device_id=ident(peer), device_id_type=MESH)

    def ag_copy(w, j, peer, slot):
        return pltpu.make_async_remote_copy(
            src_ref=share.at[w], dst_ref=full.at[w, rows_of(slot)],
            send_sem=ag_send.at[w, j], recv_sem=ag_recv.at[w, slot],
            device_id=ident(peer), device_id_type=MESH)

    def start_rs(w):
        parts[w, me] = grad[w, rows_of(me)]
        each_peer(lambda j, peer: rs_copy(w, j, peer, me).start())

    def finish_rs(w):
        each_peer(lambda j, peer: rs_copy(w, j, peer, peer).wait_recv())
        summed = lax.fori_loop(0, group, lambda i, acc: acc + parts[w, i].astype(F32),
                               jnp.zeros((chunk, 128), F32)).astype(BF16)
        share[w] = summed
        full[w, rows_of(me)] = summed
        each_peer(lambda j, peer: ag_copy(w, j, peer, me).start())

    def finish_ag(w, ref):
        each_peer(lambda j, peer: ag_copy(w, j, peer, peer).wait_recv())
        for t in range(21):
            wide = min(128, COLS - t * 128)
            ref[:, t * 128:t * 128 + wide] = full[w, t * C:(t + 1) * C].astype(F32)[:, 0:wide]

    kernel_grad(1, xb)
    start_rs(1)
    wait_halo(2)
    unfold(2, xc)

    def store_gz(p, tile, carry):
        a, b = carry
        normed = val1[p]
        z = normed * gain1 + shift1
        gz = tile * rmask[p][0:1] * silu_slope(z)
        tmp[0, p] = gz
        return a + gz, b + gz * normed
    sg, gg = run_conv(f2_ref, xc, store_gz, (zero_tile, zero_tile))
    send_back(3, sg, gg)
    finish_rs(1)
    back(3, val1, 0, gain1, inv1, finish_back(3, 0))
    send_halo(3)
    kernel_grad(0, xa)
    start_rs(0)
    wait_halo(3)
    unfold(3, xc)

    def store_fg(p, tile, carry):
        tmp[1, p] = tile * rmask[p][0:1]
        return carry
    run_conv(f1_ref, xc, store_fg, 0)
    take(tmp.at[1], fg_ref)
    finish_ag(1, wg2_ref)
    finish_rs(0)
    finish_ag(0, wg1_ref)

    for ex in range(4):
        done_halo(ex)
        done_stats(ex)
    for w in range(2):
        each_peer(lambda j, peer: rs_copy(w, j, peer, me).wait_send())
        each_peer(lambda j, peer: ag_copy(w, j, peer, me).wait_send())


def per_device(nx, ny, feats, voxel_mask, block_slot, block_count, weight_one, weight_two,
               gain_one, shift_one, gain_two, shift_two, cotangent):
    group = nx * ny
    params = jnp.pad(jnp.stack([gain_one, shift_one, gain_two, shift_two]), ((0, 4), (0, 128 - C)))
    vmem = pl.BlockSpec(memory_space=pltpu.VMEM)
    smem = pl.BlockSpec(memory_space=pltpu.SMEM)
    shapes = [
        jax.ShapeDtypeStruct((2, C, 512), BF16),
        jax.ShapeDtypeStruct((2, C, 512), BF16),
        jax.ShapeDtypeStruct((C, COLS), F32),
        jax.ShapeDtypeStruct((C, COLS), F32),
        jax.ShapeDtypeStruct((4, C), F32),
    ]
    wide = (PLANES + 2) * 128
    dma = pltpu.SemaphoreType.DMA
    return pl.pallas_call(
        functools.partial(kernel, nx, ny),
        out_shape=shapes,
        in_specs=[smem, smem] + [vmem] * 6,
        out_specs=[vmem] * 5,
        scratch_shapes=[
            pltpu.VMEM((PLANES, 8, 128), F32),
            pltpu.VMEM((4, PLANES, C, 128), BF16),
            pltpu.VMEM((PLANES, C, 128), BF16),
            pltpu.VMEM((PLANES, C, 128), F32),
            pltpu.VMEM((PLANES, C, 128), F32),
            pltpu.VMEM((2, PLANES, C, 128), F32),
            pltpu.VMEM((C, PLANES * 128), BF16),
            pltpu.VMEM((9 * C, wide), BF16),
            pltpu.VMEM((9 * C, wide), BF16),
            pltpu.VMEM((9 * C, wide), BF16),
            pltpu.VMEM((21 * 128, 128), F32),
            pltpu.VMEM((C, 21 * 128), BF16),
            pltpu.VMEM((C, 21 * 128), BF16),
            pltpu.VMEM((4, 8, C, 128), BF16),
            pltpu.VMEM((4, 2, C, 128), BF16),
            pltpu.VMEM((4, 8, 128), F32),
            pltpu.VMEM((4, group, 8, 128), F32),
            pltpu.VMEM((2, GROWS, 128), BF16),
            pltpu.VMEM((2, group, GROWS // group, 128), BF16),
            pltpu.VMEM((2, GROWS // group, 128), BF16),
            pltpu.VMEM((2, GROWS, 128), BF16),
            dma((4, 8)), dma((4, 8)),
            dma((4, group)), dma((4, group)),
            dma((2, group)), dma((2, group)),
            dma((2, group)), dma((2, group)),
        ],
        compiler_params=pltpu.CompilerParams(
            collective_id=0, has_side_effects=True, vmem_limit_bytes=48 * 1024 * 1024),
        name="section",
    )(block_slot, block_count, voxel_mask, params, feats, cotangent,
      weight_one, weight_two)


def solution(mesh):
    rows = ("scene", "gx", "gy")
    placed = (
        P(rows, None, None), P(rows, None), P(rows), P(rows),
        P(), P(), P(), P(), P(), P(), P(rows, None, None),
    )
    return jax.shard_map(
        functools.partial(per_device, mesh.shape["gx"], mesh.shape["gy"]),
        mesh=mesh,
        in_specs=placed,
        out_specs=(
            P(rows, None, None), P(rows, None, None),
            P("scene", None), P("scene", None), P("scene", None),
        ),
        check_vma=False,
    )
```

```python
import functools

import jax
import jax.numpy as jnp
from jax import lax
from jax.experimental import pallas as pl
from jax.experimental.pallas import tpu as pltpu
from jax.sharding import PartitionSpec as P

EPS = 1e-05
F32, BF16 = jnp.float32, jnp.bfloat16
MESH = pl.DeviceIdType.MESH
C = 96
PLANES = 16
SIDES = ((1, 0), (-1, 0), (0, 1), (0, -1), (1, 1), (1, -1), (-1, 1), (-1, -1))
COLS = 27 * C
TALL = C + 8
GROWS = 2048


def silu_slope(values):
    sigma = jax.nn.sigmoid(values)
    return sigma * (1.0 + values * (1.0 - sigma))


def lanes(rows=C):
    return lax.broadcasted_iota(jnp.int32, (rows, 128), 1)


def roll(tile, shift):
    return pltpu.roll(tile, shift, 1)


def kernel(nx, ny, slot_ref, count_ref, mask_ref, params_ref, feats_hbm, cot_hbm, w1_hbm, w2_hbm,
           out_ref, fg_ref, wg1_ref, wg2_ref, ng_ref,
           feats_ref, cot_ref, w1_ref, w2_ref, in_sem,
           rmask, field, cot, val1, val2, tmp, flat, xa, xb, xc, turned_w, f1_ref, f2_ref, halo, packs, edges, halo_in, packs_in, stat_src, stats,
           grad, parts, share, full,
           halo_send, halo_recv, stat_send, stat_recv, rs_send, rs_recv, ag_send, ag_recv):
    group = nx * ny
    gx, gy = lax.axis_index("gx"), lax.axis_index("gy")
    me = gx * ny + gy
    chunk = GROWS // group

    def ident(peer):
        return {"gx": peer // ny, "gy": lax.rem(peer, ny)}

    def each_peer(body):
        def step(j, carry):
            body(j, lax.rem(me + j, group))
            return carry
        lax.fori_loop(1, group, step, 0)

    loads = [pltpu.make_async_copy(src, dst, in_sem.at[i]) for i, (src, dst) in enumerate((
        (feats_hbm, feats_ref), (w2_hbm, w2_ref), (w1_hbm, w1_ref), (cot_hbm, cot_ref)))]
    for load in loads:
        load.start()
    barrier = pltpu.get_barrier_semaphore()
    each_peer(lambda j, peer: pl.semaphore_signal(
        barrier, inc=1, device_id=ident(peer), device_id_type=MESH))

    live = [(k < count_ref[0]).astype(F32) for k in range(2)]
    hot = [[(slot_ref[k] == s).astype(F32) for s in range(4)] for k in range(2)]

    def place(tile_of, rows, store):
        low = lanes(rows) < 64
        for t in range(4):
            tiles = [tile_of(k, t) for k in range(2)]
            turned = [roll(x, 64) for x in tiles]
            for sx in range(2):
                first = sum(jnp.where(low, hot[k][2 * sx] * tiles[k], hot[k][2 * sx + 1] * turned[k])
                            for k in range(2))
                second = sum(jnp.where(low, hot[k][2 * sx] * turned[k], hot[k][2 * sx + 1] * tiles[k])
                             for k in range(2))
                store(sx * 8 + 2 * t, first)
                store(sx * 8 + 2 * t + 1, second)

    def take(src, ref):
        low = lanes() < 64
        for t in range(4):
            acc = [jnp.zeros((C, 128), F32) for _ in range(2)]
            for sx in range(2):
                a, b = src[sx * 8 + 2 * t], src[sx * 8 + 2 * t + 1]
                left = jnp.where(low, a, roll(b, 64))
                right = jnp.where(low, roll(a, 64), b)
                for k in range(2):
                    acc[k] = acc[k] + hot[k][2 * sx] * left + hot[k][2 * sx + 1] * right
            for k in range(2):
                ref[k, :, t * 128:(t + 1) * 128] = acc[k].astype(BF16)

    def store_mask(p, value):
        rmask[p] = value

    def store_input(p, value):
        field[0, p] = (value * rmask[p][0:1]).astype(BF16)

    def store_cot(p, value):
        cot[p] = (value * rmask[p][0:1]).astype(BF16)

    place(lambda k, t: jnp.broadcast_to(
        mask_ref[k:k + 1, t * 128:(t + 1) * 128].astype(F32) * live[k], (8, 128)), 8, store_mask)
    loads[0].wait()
    place(lambda k, t: feats_ref[k, :, t * 128:(t + 1) * 128].astype(F32), C, store_input)

    planes_of = [field.at[0], val1, val2, tmp.at[1], tmp.at[2]]
    rows_in = [C, TALL, C, C, C]

    def landing(ex, d):
        return halo_in.at[d] if ex == 0 else halo.at[ex - 1, d, 0:rows_in[ex]]

    def packed(ex, h):
        return packs_in.at[h] if ex == 0 else packs.at[ex - 1, h, 0:rows_in[ex]]

    def halo_copy(ex, d):
        dx, dy = SIDES[d]
        if dx == 0:
            src = packed(ex, 0 if dy == 1 else 1)
        else:
            src = planes_of[ex].at[PLANES - 1 if dx == 1 else 0]
        return pltpu.make_async_remote_copy(
            src_ref=src, dst_ref=landing(ex, d),
            send_sem=halo_send.at[ex, d], recv_sem=halo_recv.at[ex, d],
            device_id={"gx": gx + dx, "gy": gy + dy}, device_id_type=MESH)

    def inside(dx, dy):
        return (gx + dx >= 0) & (gx + dx < nx) & (gy + dy >= 0) & (gy + dy < ny)

    for d, (dx, dy) in enumerate(SIDES):
        @pl.when(jnp.logical_not(inside(-dx, -dy)))
        def _(d=d):
            halo_in[d] = jnp.zeros((C, 128), BF16)
            for ex in range(4):
                halo[ex, d] = jnp.zeros((TALL, 128), F32)

    def send_halo(ex):
        rows = rows_in[ex]
        lane = lanes(rows)

        def pack(i, carry):
            high, low = carry
            plane = planes_of[ex][i].astype(F32)
            here = (lane >= i * 8) & (lane < i * 8 + 8)
            high = jnp.where(here, roll(plane, lax.rem(i * 8 + 8, 128)), high)
            low = jnp.where(here, roll(plane, i * 8), low)
            return high, low

        zero = jnp.zeros((rows, 128), F32)
        high, low = lax.fori_loop(0, PLANES, pack, (zero, zero))
        kind = BF16 if ex == 0 else F32
        packed(ex, 0)[...] = high.astype(kind)
        packed(ex, 1)[...] = low.astype(kind)
        for d, (dx, dy) in enumerate(SIDES):
            @pl.when(inside(dx, dy))
            def _(d=d):
                halo_copy(ex, d).start()

    def wait_halo(ex):
        for d, (dx, dy) in enumerate(SIDES):
            @pl.when(inside(-dx, -dy))
            def _(d=d):
                halo_copy(ex, d).wait_recv()

    def done_halo(ex):
        for d, (dx, dy) in enumerate(SIDES):
            @pl.when(inside(dx, dy))
            def _(d=d):
                halo_copy(ex, d).wait_send()

    def side(near, dx, dy):
        return near[SIDES.index((-dx, -dy))].astype(F32)

    def spread(x, p, plane, edge):
        lane = lanes()
        z = lane % 8
        for oy in (-1, 0, 1):
            src = plane
            if oy == 1:
                src = jnp.where(lane < 8, edge, plane)
            elif oy == -1:
                src = jnp.where(lane >= 120, edge, plane)
            for oz in (-1, 0, 1):
                shift = (-(8 * oy + oz)) % 128
                r = roll(src, shift) if shift else src
                if oz == 1:
                    r = jnp.where(z < 7, r, 0.0)
                elif oz == -1:
                    r = jnp.where(z > 0, r, 0.0)
                row = ((oy + 1) * 3 + oz + 1) * C
                start = p * 128 if isinstance(p, int) else pl.multiple_of(p * 128, 128)
                x[row:row + C, pl.ds(start, 128)] = r.astype(BF16)

    def unfold(ex, x):
        lane = lanes()
        near = halo_in if ex == 0 else edges
        for p, dx in ((0, -1), (PLANES + 1, 1)):
            edge = jnp.where(lane < 64, side(near, dx, 1), side(near, dx, -1))
            spread(x, p, side(near, dx, 0), edge)

        def body(i, carry):
            before = roll(side(near, 0, -1), lax.rem(248 - i * 8, 128))
            after = roll(side(near, 0, 1), lax.rem(128 - i * 8, 128))
            spread(x, i + 1, field[ex, i].astype(F32), jnp.where(lane < 64, after, before))
            return carry
        lax.fori_loop(0, PLANES, body, 0)

    def slabs():
        return [(lo, min(lo + 256, COLS)) for lo in range(0, COLS, 256)]

    def pieces_of(lo, hi):
        found = []
        for ox in range(3):
            first, last = max(lo, ox * 9 * C), min(hi, (ox + 1) * 9 * C)
            if first < last:
                found.append((ox, first - ox * 9 * C, last - ox * 9 * C))
        return found

    def joined(pieces):
        return pieces[0] if len(pieces) == 1 else jnp.concatenate(pieces, axis=0)

    def flip(w_ref, out):
        for lo in range(0, COLS, 128):
            wide = min(128, COLS - lo)
            tile = w_ref[:, lo:lo + wide].astype(F32)
            if wide < 128:
                tile = jnp.concatenate([tile, jnp.zeros((C, 128 - wide), F32)], axis=1)
            tile = jnp.concatenate([tile, jnp.zeros((128 - C, 128), F32)], axis=0)
            turned_w[lo:lo + 128] = jnp.transpose(tile)
        lane = lanes()
        for lo in range(0, COLS, 128):
            tile = jnp.zeros((C, 128), F32)
            for o in range(27):
                to = o * C - lo
                if to < 128 and to + C > 0:
                    block = turned_w[(26 - o) * C:(27 - o) * C]
                    block = roll(block, to % 128) if to % 128 else block
                    tile = jnp.where((lane >= to) & (lane < to + C), block, tile)
            out[:, lo:lo + 128] = tile.astype(BF16)

    def conv(w_ref, x, store):
        def body(j, carry):
            acc = None
            for lo, hi in slabs():
                cols = [x[a:b, pl.ds(pl.multiple_of((2 * j + ox) * 128, 128), 256)]
                        for ox, a, b in pieces_of(lo, hi)]
                part = jnp.dot(w_ref[:, lo:hi], joined(cols), preferred_element_type=F32)
                acc = part if acc is None else acc + part
            for h in range(2):
                carry = store(2 * j + h, acc[:, h * 128:(h + 1) * 128], carry)
            return carry
        return body

    def run_conv(w_ref, x, store, init):
        return lax.fori_loop(0, PLANES // 2, conv(w_ref, x, store), init)

    def pack_columns(columns):
        lane = lanes(C)
        tile = jnp.zeros((C, 128), F32)
        for i, column in enumerate(columns):
            tile = jnp.where(lane == i, column, tile)
        whole = jnp.concatenate([tile, jnp.zeros((128 - C, 128), F32)], axis=0)
        return jnp.transpose(whole)[0:8]

    def to_columns(rows):
        whole = jnp.concatenate(rows + [jnp.zeros((128 - len(rows), 128), F32)], axis=0)
        turned = jnp.transpose(whole)
        return [turned[0:C, i:i + 1] for i in range(len(rows))]

    def stat_copy(ph, j, peer, slot):
        return pltpu.make_async_remote_copy(
            src_ref=stat_src.at[ph], dst_ref=stats.at[ph, slot],
            send_sem=stat_send.at[ph, j], recv_sem=stat_recv.at[ph, slot],
            device_id=ident(peer), device_id_type=MESH)

    def send_stats(ph, tile):
        stat_src[ph] = tile
        stats[ph, me] = tile
        each_peer(lambda j, peer: stat_copy(ph, j, peer, me).start())

    def wait_stats(ph):
        each_peer(lambda j, peer: stat_copy(ph, j, peer, peer).wait_recv())

    def done_stats(ph):
        each_peer(lambda j, peer: stat_copy(ph, j, peer, me).wait_send())

    def total_stats(ph):
        return lax.fori_loop(0, group, lambda i, acc: acc + stats[ph, i], jnp.zeros((8, 128), F32))

    def total(tile):
        return jnp.sum(tile, axis=1, keepdims=True)

    zero_tile = jnp.zeros((C, 128), F32)
    here = lax.fori_loop(0, PLANES, lambda i, acc: acc + rmask[i], jnp.zeros((8, 128), F32))
    here = jnp.sum(here[0:1], axis=1, keepdims=True)

    def moments(ph, val, summed):
        mean = total(summed) / jnp.maximum(here, 1.0)

        def body(i, acc):
            centred = (val[i, 0:C] - mean) * rmask[i][0:1]
            return acc + centred * centred
        spread_sum = total(lax.fori_loop(0, PLANES, body, zero_tile))
        send_stats(ph, pack_columns([total(summed), spread_sum, jnp.broadcast_to(here, (C, 1))]))
        wait_stats(ph)
        sums = total_stats(ph)
        count = jnp.maximum(jnp.max(sums[2:3], axis=1, keepdims=True), 1.0)
        mean_row = sums[0:1] / count

        def shifted(i, acc):
            tile = stats[ph, i]
            n = tile[2:3]
            gap = tile[0:1] / jnp.maximum(n, 1.0) - mean_row
            return acc + tile[1:2] + n * gap * gap
        square = lax.fori_loop(0, group, shifted, jnp.zeros((1, 128), F32))
        inv_row = lax.rsqrt(square / count + EPS)
        mean_col, inv_col = to_columns([mean_row, inv_row])
        return mean_col, inv_col, 1.0 / count

    def store_conv(val):
        def store(p, tile, acc):
            y = tile * rmask[p][0:1]
            val[p, 0:C] = y
            return acc + y
        return store

    gain1, shift1, gain2, shift2 = to_columns([params_ref[i:i + 1] for i in range(4)])

    pl.semaphore_wait(barrier, group - 1)
    send_halo(0)

    def mask_rows(i, carry):
        val1[i, C:TALL] = rmask[i]
        return carry
    lax.fori_loop(0, PLANES, mask_rows, 0)
    for load in loads[1:]:
        load.wait()
    place(lambda k, t: cot_ref[k, :, t * 128:(t + 1) * 128].astype(F32), C, store_cot)
    flip(w2_ref, f2_ref)
    flip(w1_ref, f1_ref)
    wait_halo(0)
    unfold(0, xa)
    summed = run_conv(w1_ref, xa, store_conv(val1), zero_tile)
    send_halo(1)
    mean1, inv1, per = moments(0, val1, summed)

    def near_mask(d):
        return halo[0, d, C:C + 1]

    def norm_one(y, m):
        return (y - mean1) * m * inv1

    def active(y, m):
        z = norm_one(y, m) * gain1 + shift1
        return (z * jax.nn.sigmoid(z) * m).astype(BF16)

    def act_one(i, carry):
        field[1, i] = active(val1[i, 0:C], rmask[i][0:1])
        return carry
    lax.fori_loop(0, PLANES, act_one, 0)
    wait_halo(1)

    def edge_one(d, carry):
        edges[d] = active(halo[0, d, 0:C], near_mask(d))
        return carry
    lax.fori_loop(0, 8, edge_one, 0)

    unfold(1, xb)
    summed = run_conv(w2_ref, xb, store_conv(val2), zero_tile)
    send_halo(2)
    mean2, inv2, per = moments(1, val2, summed)

    def norm_two(y, m):
        return (y - mean2) * m * inv2

    def act_two(i, carry):
        a, b = carry
        m = rmask[i][0:1]
        normed = norm_two(val2[i], m)
        z = normed * gain2 + shift2
        sigma = jax.nn.sigmoid(z)
        tmp[0, i] = z * sigma * m
        gz = cot[i].astype(F32) * (sigma * (1.0 + z * (1.0 - sigma)))
        tmp[1, i] = gz
        return a + gz, b + gz * normed
    sg, gg = lax.fori_loop(0, PLANES, act_two, (zero_tile, zero_tile))

    def send_back(ph, sg, gg):
        send_stats(ph, pack_columns([total(sg), total(gg)]))

    def finish_back(ph, row):
        wait_stats(ph)
        sums = total_stats(ph)
        ng_ref[row:row + 1, :] = sums[1:2, 0:C]
        ng_ref[row + 1:row + 2, :] = sums[0:1, 0:C]
        return to_columns([sums[0:1], sums[1:2]])

    def back(ex, val, gz_slot, near_val, norm, gain, inv, sums):
        sg, gg = sums[0] * per, sums[1] * per
        scaled = gain * inv

        def slope(gz, y, m):
            return (m * scaled * (gz - sg - norm(y, m) * gg)).astype(BF16)

        def body(i, carry):
            g = slope(tmp[gz_slot, i], val[i, 0:C], rmask[i][0:1])
            field[ex, i] = g
            flat[:, pl.ds(pl.multiple_of(i * 128, 128), 128)] = g
            return carry
        lax.fori_loop(0, PLANES, body, 0)
        wait_halo(ex + 1)

        def edge(d, carry):
            edges[d] = slope(halo[ex, d, 0:C], halo[near_val, d, 0:C], near_mask(d))
            return carry
        lax.fori_loop(0, 8, edge, 0)

    send_back(2, sg, gg)
    send_halo(3)
    take(tmp.at[0], out_ref)
    wait_halo(2)
    back(2, val2, 1, 1, norm_two, gain2, inv2, finish_back(2, 2))

    def kernel_grad(w, x):
        for lo, hi in slabs():
            rhs = joined([x[a:b, ox * 128:ox * 128 + PLANES * 128]
                          for ox, a, b in pieces_of(lo, hi)])
            part = lax.dot_general(flat[...], rhs, (((1,), (1,)), ((), ())),
                                   preferred_element_type=F32).astype(BF16)
            for h in range(0, hi - lo, 128):
                tile = part[:, h:min(h + 128, hi - lo)]
                if tile.shape[1] < 128:
                    tile = jnp.concatenate(
                        [tile, jnp.zeros((C, 128 - tile.shape[1]), BF16)], axis=1)
                row = (lo + h) // 128 * C
                grad[w, row:row + C] = tile
        grad[w, 21 * C:GROWS] = jnp.zeros((GROWS - 21 * C, 128), BF16)

    def rows_of(i):
        return pl.ds(pl.multiple_of(i * chunk, chunk), chunk)

    def rs_copy(w, j, peer, slot):
        return pltpu.make_async_remote_copy(
            src_ref=grad.at[w, rows_of(peer)], dst_ref=parts.at[w, slot],
            send_sem=rs_send.at[w, j], recv_sem=rs_recv.at[w, slot],
            device_id=ident(peer), device_id_type=MESH)

    def ag_copy(w, j, peer, slot):
        return pltpu.make_async_remote_copy(
            src_ref=share.at[w], dst_ref=full.at[w, rows_of(slot)],
            send_sem=ag_send.at[w, j], recv_sem=ag_recv.at[w, slot],
            device_id=ident(peer), device_id_type=MESH)

    def start_rs(w):
        parts[w, me] = grad[w, rows_of(me)]
        each_peer(lambda j, peer: rs_copy(w, j, peer, me).start())

    def finish_rs(w):
        each_peer(lambda j, peer: rs_copy(w, j, peer, peer).wait_recv())
        summed = lax.fori_loop(0, group, lambda i, acc: acc + parts[w, i].astype(F32),
                               jnp.zeros((chunk, 128), F32)).astype(BF16)
        share[w] = summed
        full[w, rows_of(me)] = summed
        each_peer(lambda j, peer: ag_copy(w, j, peer, me).start())

    def finish_ag(w, ref):
        each_peer(lambda j, peer: ag_copy(w, j, peer, peer).wait_recv())
        for t in range(21):
            wide = min(128, COLS - t * 128)
            ref[:, t * 128:t * 128 + wide] = full[w, t * C:(t + 1) * C].astype(F32)[:, 0:wide]

    kernel_grad(1, xb)
    start_rs(1)
    unfold(2, xc)

    def store_gz(p, tile, carry):
        a, b = carry
        normed = norm_one(val1[p, 0:C], rmask[p][0:1])
        z = normed * gain1 + shift1
        gz = tile * rmask[p][0:1] * silu_slope(z)
        tmp[2, p] = gz
        return a + gz, b + gz * normed
    sg, gg = run_conv(f2_ref, xc, store_gz, (zero_tile, zero_tile))
    send_back(3, sg, gg)
    send_halo(4)
    finish_rs(1)
    back(3, val1, 2, 0, norm_one, gain1, inv1, finish_back(3, 0))
    kernel_grad(0, xa)
    start_rs(0)
    unfold(3, xc)

    def store_fg(p, tile, carry):
        tmp[0, p] = tile * rmask[p][0:1]
        return carry
    run_conv(f1_ref, xc, store_fg, 0)
    take(tmp.at[0], fg_ref)
    finish_ag(1, wg2_ref)
    finish_rs(0)
    finish_ag(0, wg1_ref)

    for ex in range(5):
        done_halo(ex)
    for ph in range(4):
        done_stats(ph)
    for w in range(2):
        each_peer(lambda j, peer: rs_copy(w, j, peer, me).wait_send())
        each_peer(lambda j, peer: ag_copy(w, j, peer, me).wait_send())


def per_device(nx, ny, feats, voxel_mask, block_slot, block_count, weight_one, weight_two,
               gain_one, shift_one, gain_two, shift_two, cotangent):
    group = nx * ny
    params = jnp.pad(jnp.stack([gain_one, shift_one, gain_two, shift_two]), ((0, 4), (0, 128 - C)))
    vmem = pl.BlockSpec(memory_space=pltpu.VMEM)
    smem = pl.BlockSpec(memory_space=pltpu.SMEM)
    shapes = [
        jax.ShapeDtypeStruct((2, C, 512), BF16),
        jax.ShapeDtypeStruct((2, C, 512), BF16),
        jax.ShapeDtypeStruct((C, COLS), F32),
        jax.ShapeDtypeStruct((C, COLS), F32),
        jax.ShapeDtypeStruct((4, C), F32),
    ]
    wide = (PLANES + 2) * 128
    dma = pltpu.SemaphoreType.DMA
    return pl.pallas_call(
        functools.partial(kernel, nx, ny),
        out_shape=shapes,
        in_specs=[smem, smem] + [vmem] * 2 + [pl.BlockSpec(memory_space=pl.ANY)] * 4,
        out_specs=[vmem] * 5,
        scratch_shapes=[
            pltpu.VMEM((2, C, 512), BF16),
            pltpu.VMEM((2, C, 512), BF16),
            pltpu.VMEM((C, COLS), BF16),
            pltpu.VMEM((C, COLS), BF16),
            dma((4,)),
            pltpu.VMEM((PLANES, 8, 128), F32),
            pltpu.VMEM((4, PLANES, C, 128), BF16),
            pltpu.VMEM((PLANES, C, 128), BF16),
            pltpu.VMEM((PLANES, TALL, 128), F32),
            pltpu.VMEM((PLANES, C, 128), F32),
            pltpu.VMEM((3, PLANES, C, 128), F32),
            pltpu.VMEM((C, PLANES * 128), BF16),
            pltpu.VMEM((9 * C, wide), BF16),
            pltpu.VMEM((9 * C, wide), BF16),
            pltpu.VMEM((9 * C, wide), BF16),
            pltpu.VMEM((21 * 128, 128), F32),
            pltpu.VMEM((C, 21 * 128), BF16),
            pltpu.VMEM((C, 21 * 128), BF16),
            pltpu.VMEM((4, 8, TALL, 128), F32),
            pltpu.VMEM((4, 2, TALL, 128), F32),
            pltpu.VMEM((8, C, 128), BF16),
            pltpu.VMEM((8, C, 128), BF16),
            pltpu.VMEM((2, C, 128), BF16),
            pltpu.VMEM((4, 8, 128), F32),
            pltpu.VMEM((4, group, 8, 128), F32),
            pltpu.VMEM((2, GROWS, 128), BF16),
            pltpu.VMEM((2, group, GROWS // group, 128), BF16),
            pltpu.VMEM((2, GROWS // group, 128), BF16),
            pltpu.VMEM((2, GROWS, 128), BF16),
            dma((5, 8)), dma((5, 8)),
            dma((4, group)), dma((4, group)),
            dma((2, group)), dma((2, group)),
            dma((2, group)), dma((2, group)),
        ],
        compiler_params=pltpu.CompilerParams(
            collective_id=0, has_side_effects=True, vmem_limit_bytes=60 * 1024 * 1024),
        name="section",
    )(block_slot, block_count, voxel_mask, params, feats, cotangent,
      weight_one, weight_two)


def solution(mesh):
    rows = ("scene", "gx", "gy")
    placed = (
        P(rows, None, None), P(rows, None), P(rows), P(rows),
        P(), P(), P(), P(), P(), P(), P(rows, None, None),
    )
    return jax.shard_map(
        functools.partial(per_device, mesh.shape["gx"], mesh.shape["gy"]),
        mesh=mesh,
        in_specs=placed,
        out_specs=(
            P(rows, None, None), P(rows, None, None),
            P("scene", None), P("scene", None), P("scene", None),
        ),
        check_vma=False,
    )
```

```python
import functools

import jax
import jax.numpy as jnp
from jax import lax
from jax.experimental import pallas as pl
from jax.experimental.pallas import tpu as pltpu
from jax.sharding import PartitionSpec as P

EPS = 1e-05
F32, BF16 = jnp.float32, jnp.bfloat16
MESH = pl.DeviceIdType.MESH
C = 96
PLANES = 16
SIDES = ((1, 0), (-1, 0), (0, 1), (0, -1), (1, 1), (1, -1), (-1, 1), (-1, -1))
COLS = 27 * C
TALL = C + 8
GROWS = 2048


def silu_slope(values):
    sigma = jax.nn.sigmoid(values)
    return sigma * (1.0 + values * (1.0 - sigma))


def lanes(rows=C):
    return lax.broadcasted_iota(jnp.int32, (rows, 128), 1)


def roll(tile, shift):
    return pltpu.roll(tile, shift, 1)


def kernel(nx, ny, slot_ref, count_ref, mask_ref, params_ref, feats_hbm, cot_hbm, w1_hbm, w2_hbm,
           out_ref, fg_ref, wg1_ref, wg2_ref, ng_ref,
           feats_ref, cot_ref, w1_ref, w2_ref, in_sem,
           rmask, field, cot, val1, val2, tmp, flat, xa, xb, xc, turned_w, f1_ref, f2_ref, halo, packs, edges, halo_in, packs_in, corner_src, corner_in, stat_src, stats,
           grad, parts, share, full,
           halo_send, halo_recv, stat_send, stat_recv, rs_send, rs_recv, ag_send, ag_recv):
    group = nx * ny
    gx, gy = lax.axis_index("gx"), lax.axis_index("gy")
    me = gx * ny + gy
    chunk = GROWS // group

    def ident(peer):
        return {"gx": peer // ny, "gy": lax.rem(peer, ny)}

    def each_peer(body):
        def step(j, carry):
            body(j, lax.rem(me + j, group))
            return carry
        lax.fori_loop(1, group, step, 0)

    loads = [pltpu.make_async_copy(src, dst, in_sem.at[i]) for i, (src, dst) in enumerate((
        (feats_hbm, feats_ref), (w2_hbm, w2_ref), (w1_hbm, w1_ref), (cot_hbm, cot_ref)))]
    for load in loads:
        load.start()
    barrier = pltpu.get_barrier_semaphore()
    each_peer(lambda j, peer: pl.semaphore_signal(
        barrier, inc=1, device_id=ident(peer), device_id_type=MESH))

    live = [(k < count_ref[0]).astype(F32) for k in range(2)]
    hot = [[(slot_ref[k] == s).astype(F32) for s in range(4)] for k in range(2)]

    def place(tile_of, rows, store):
        low = lanes(rows) < 64
        for t in range(4):
            tiles = [tile_of(k, t) for k in range(2)]
            turned = [roll(x, 64) for x in tiles]
            for sx in range(2):
                first = sum(jnp.where(low, hot[k][2 * sx] * tiles[k], hot[k][2 * sx + 1] * turned[k])
                            for k in range(2))
                second = sum(jnp.where(low, hot[k][2 * sx] * turned[k], hot[k][2 * sx + 1] * tiles[k])
                             for k in range(2))
                store(sx * 8 + 2 * t, first)
                store(sx * 8 + 2 * t + 1, second)

    def take(src, ref):
        low = lanes() < 64
        for t in range(4):
            acc = [jnp.zeros((C, 128), F32) for _ in range(2)]
            for sx in range(2):
                a, b = src[sx * 8 + 2 * t], src[sx * 8 + 2 * t + 1]
                left = jnp.where(low, a, roll(b, 64))
                right = jnp.where(low, roll(a, 64), b)
                for k in range(2):
                    acc[k] = acc[k] + hot[k][2 * sx] * left + hot[k][2 * sx + 1] * right
            for k in range(2):
                ref[k, :, t * 128:(t + 1) * 128] = acc[k].astype(BF16)

    def store_mask(p, value):
        rmask[p] = value

    def store_input(p, value):
        field[0, p] = (value * rmask[p][0:1]).astype(BF16)

    def store_cot(p, value):
        cot[p] = (value * rmask[p][0:1]).astype(BF16)

    place(lambda k, t: jnp.broadcast_to(
        mask_ref[k:k + 1, t * 128:(t + 1) * 128].astype(F32) * live[k], (8, 128)), 8, store_mask)
    loads[0].wait()
    place(lambda k, t: feats_ref[k, :, t * 128:(t + 1) * 128].astype(F32), C, store_input)

    planes_of = [field.at[0], val1, val2, tmp.at[1], tmp.at[2]]
    rows_in = [C, TALL, C, C, C]

    def landing(ex, d):
        if d >= 4:
            return corner_in.at[ex, d - 4]
        return halo_in.at[d] if ex == 0 else halo.at[ex - 1, d, 0:rows_in[ex]]

    def packed(ex, h):
        return packs_in.at[h] if ex == 0 else packs.at[ex - 1, h, 0:rows_in[ex]]

    def halo_copy(ex, d):
        dx, dy = SIDES[d]
        if d >= 4:
            src = corner_src.at[ex, d - 4]
        elif dx == 0:
            src = packed(ex, 0 if dy == 1 else 1)
        else:
            src = planes_of[ex].at[PLANES - 1 if dx == 1 else 0]
        return pltpu.make_async_remote_copy(
            src_ref=src, dst_ref=landing(ex, d),
            send_sem=halo_send.at[ex, d], recv_sem=halo_recv.at[ex, d],
            device_id={"gx": gx + dx, "gy": gy + dy}, device_id_type=MESH)

    def inside(dx, dy):
        return (gx + dx >= 0) & (gx + dx < nx) & (gy + dy >= 0) & (gy + dy < ny)

    for d, (dx, dy) in enumerate(SIDES):
        @pl.when(jnp.logical_not(inside(-dx, -dy)))
        def _(d=d):
            if d >= 4:
                for ex in range(5):
                    corner_in[ex, d - 4] = jnp.zeros((8, 128), F32)
                return
            halo_in[d] = jnp.zeros((C, 128), BF16)
            for ex in range(4):
                halo[ex, d] = jnp.zeros((TALL, 128), F32)

    def send_halo(ex):
        rows = rows_in[ex]
        lane = lanes(rows)

        for dx in (1, -1):
            plane = planes_of[ex][PLANES - 1 if dx == 1 else 0].astype(F32)
            turned = jnp.transpose(jnp.concatenate(
                [plane, jnp.zeros((128 - rows, 128), F32)], axis=0))
            corner_src[ex, SIDES.index((dx, 1)) - 4] = turned[120:128]
            corner_src[ex, SIDES.index((dx, -1)) - 4] = turned[0:8]

        high = low = jnp.zeros((rows, 128), F32)
        for i in range(PLANES):
            plane = planes_of[ex][i].astype(F32)
            here = (lane >= i * 8) & (lane < i * 8 + 8)
            to_high, to_low = (i * 8 + 8) % 128, i * 8
            high = jnp.where(here, roll(plane, to_high) if to_high else plane, high)
            low = jnp.where(here, roll(plane, to_low) if to_low else plane, low)
        kind = BF16 if ex == 0 else F32
        packed(ex, 0)[...] = high.astype(kind)
        packed(ex, 1)[...] = low.astype(kind)
        for d, (dx, dy) in enumerate(SIDES):
            @pl.when(inside(dx, dy))
            def _(d=d):
                halo_copy(ex, d).start()

    def wait_halo(ex):
        for d, (dx, dy) in enumerate(SIDES):
            @pl.when(inside(-dx, -dy))
            def _(d=d):
                halo_copy(ex, d).wait_recv()
        for slot, dx in ((4, -1), (5, 1)):
            after = corner_in[ex, SIDES.index((-dx, -1)) - 4]
            before = corner_in[ex, SIDES.index((-dx, 1)) - 4]
            tile = jnp.transpose(jnp.concatenate(
                [after, jnp.zeros((112, 128), F32), before], axis=0))
            if ex == 0:
                halo_in[slot] = tile[0:C].astype(BF16)
            else:
                halo[ex - 1, slot] = tile[0:TALL]

    def done_halo(ex):
        for d, (dx, dy) in enumerate(SIDES):
            @pl.when(inside(dx, dy))
            def _(d=d):
                halo_copy(ex, d).wait_send()

    def side(near, dx, dy):
        return near[SIDES.index((-dx, -dy))].astype(F32)

    def spread(x, p, plane, edge):
        lane = lanes()
        z = lane % 8
        for oy in (-1, 0, 1):
            src = plane
            if oy == 1:
                src = jnp.where(lane < 8, edge, plane)
            elif oy == -1:
                src = jnp.where(lane >= 120, edge, plane)
            for oz in (-1, 0, 1):
                shift = (-(8 * oy + oz)) % 128
                r = roll(src, shift) if shift else src
                if oz == 1:
                    r = jnp.where(z < 7, r, 0.0)
                elif oz == -1:
                    r = jnp.where(z > 0, r, 0.0)
                row = ((oy + 1) * 3 + oz + 1) * C
                start = p * 128 if isinstance(p, int) else pl.multiple_of(p * 128, 128)
                x[row:row + C, pl.ds(start, 128)] = r.astype(BF16)

    def unfold(ex, x):
        lane = lanes()
        near = halo_in if ex == 0 else edges
        for p, dx in ((0, -1), (PLANES + 1, 1)):
            edge = near[4 if dx == -1 else 5].astype(F32)
            spread(x, p, side(near, dx, 0), edge)

        def body(i, carry):
            before = roll(side(near, 0, -1), lax.rem(248 - i * 8, 128))
            after = roll(side(near, 0, 1), lax.rem(128 - i * 8, 128))
            spread(x, i + 1, field[ex, i].astype(F32), jnp.where(lane < 64, after, before))
            return carry
        lax.fori_loop(0, PLANES, body, 0)

    def slabs():
        return [(lo, min(lo + 256, COLS)) for lo in range(0, COLS, 256)]

    def pieces_of(lo, hi):
        found = []
        for ox in range(3):
            first, last = max(lo, ox * 9 * C), min(hi, (ox + 1) * 9 * C)
            if first < last:
                found.append((ox, first - ox * 9 * C, last - ox * 9 * C))
        return found

    def joined(pieces):
        return pieces[0] if len(pieces) == 1 else jnp.concatenate(pieces, axis=0)

    def flip(w_ref, out):
        for lo in range(0, COLS, 128):
            wide = min(128, COLS - lo)
            tile = w_ref[:, lo:lo + wide].astype(F32)
            if wide < 128:
                tile = jnp.concatenate([tile, jnp.zeros((C, 128 - wide), F32)], axis=1)
            tile = jnp.concatenate([tile, jnp.zeros((128 - C, 128), F32)], axis=0)
            turned_w[lo:lo + 128] = jnp.transpose(tile)
        lane = lanes()
        for lo in range(0, COLS, 128):
            tile = jnp.zeros((C, 128), F32)
            for o in range(27):
                to = o * C - lo
                if to < 128 and to + C > 0:
                    block = turned_w[(26 - o) * C:(27 - o) * C]
                    block = roll(block, to % 128) if to % 128 else block
                    tile = jnp.where((lane >= to) & (lane < to + C), block, tile)
            out[:, lo:lo + 128] = tile.astype(BF16)

    def conv(w_ref, x, store):
        def body(j, carry):
            acc = None
            for lo, hi in slabs():
                cols = [x[a:b, pl.ds(pl.multiple_of((2 * j + ox) * 128, 128), 256)]
                        for ox, a, b in pieces_of(lo, hi)]
                part = jnp.dot(w_ref[:, lo:hi], joined(cols), preferred_element_type=F32)
                acc = part if acc is None else acc + part
            for h in range(2):
                carry = store(2 * j + h, acc[:, h * 128:(h + 1) * 128], carry)
            return carry
        return body

    def run_conv(w_ref, x, store, init):
        return lax.fori_loop(0, PLANES // 2, conv(w_ref, x, store), init)

    def pack_columns(columns):
        lane = lanes(C)
        tile = jnp.zeros((C, 128), F32)
        for i, column in enumerate(columns):
            tile = jnp.where(lane == i, column, tile)
        whole = jnp.concatenate([tile, jnp.zeros((128 - C, 128), F32)], axis=0)
        return jnp.transpose(whole)[0:8]

    def to_columns(rows):
        whole = jnp.concatenate(rows + [jnp.zeros((128 - len(rows), 128), F32)], axis=0)
        turned = jnp.transpose(whole)
        return [turned[0:C, i:i + 1] for i in range(len(rows))]

    def stat_copy(ph, j, peer, slot):
        return pltpu.make_async_remote_copy(
            src_ref=stat_src.at[ph], dst_ref=stats.at[ph, slot],
            send_sem=stat_send.at[ph, j], recv_sem=stat_recv.at[ph, slot],
            device_id=ident(peer), device_id_type=MESH)

    def send_stats(ph, tile):
        stat_src[ph] = tile
        stats[ph, me] = tile
        each_peer(lambda j, peer: stat_copy(ph, j, peer, me).start())

    def wait_stats(ph):
        each_peer(lambda j, peer: stat_copy(ph, j, peer, peer).wait_recv())

    def done_stats(ph):
        each_peer(lambda j, peer: stat_copy(ph, j, peer, me).wait_send())

    def total_stats(ph):
        return lax.fori_loop(0, group, lambda i, acc: acc + stats[ph, i], jnp.zeros((8, 128), F32))

    def total(tile):
        return jnp.sum(tile, axis=1, keepdims=True)

    zero_tile = jnp.zeros((C, 128), F32)
    here = lax.fori_loop(0, PLANES, lambda i, acc: acc + rmask[i], jnp.zeros((8, 128), F32))
    here = jnp.sum(here[0:1], axis=1, keepdims=True)

    def moments(ph, val, summed):
        mean = total(summed) / jnp.maximum(here, 1.0)

        def body(i, acc):
            centred = (val[i, 0:C] - mean) * rmask[i][0:1]
            return acc + centred * centred
        spread_sum = total(lax.fori_loop(0, PLANES, body, zero_tile))
        send_stats(ph, pack_columns([total(summed), spread_sum, jnp.broadcast_to(here, (C, 1))]))
        wait_stats(ph)
        sums = total_stats(ph)
        count = jnp.maximum(jnp.max(sums[2:3], axis=1, keepdims=True), 1.0)
        mean_row = sums[0:1] / count

        def shifted(i, acc):
            tile = stats[ph, i]
            n = tile[2:3]
            gap = tile[0:1] / jnp.maximum(n, 1.0) - mean_row
            return acc + tile[1:2] + n * gap * gap
        square = lax.fori_loop(0, group, shifted, jnp.zeros((1, 128), F32))
        inv_row = lax.rsqrt(square / count + EPS)
        mean_col, inv_col = to_columns([mean_row, inv_row])
        return mean_col, inv_col, 1.0 / count

    def store_conv(val):
        def store(p, tile, acc):
            y = tile * rmask[p][0:1]
            val[p, 0:C] = y
            return acc + y
        return store

    gain1, shift1, gain2, shift2 = to_columns([params_ref[i:i + 1] for i in range(4)])

    pl.semaphore_wait(barrier, group - 1)
    send_halo(0)

    def mask_rows(i, carry):
        val1[i, C:TALL] = rmask[i]
        return carry
    lax.fori_loop(0, PLANES, mask_rows, 0)
    for load in loads[1:]:
        load.wait()
    place(lambda k, t: cot_ref[k, :, t * 128:(t + 1) * 128].astype(F32), C, store_cot)
    flip(w2_ref, f2_ref)
    flip(w1_ref, f1_ref)
    wait_halo(0)
    unfold(0, xa)
    summed = run_conv(w1_ref, xa, store_conv(val1), zero_tile)
    send_halo(1)
    mean1, inv1, per = moments(0, val1, summed)

    def near_mask(d):
        return halo[0, d, C:C + 1]

    def norm_one(y, m):
        return (y - mean1) * m * inv1

    def active(y, m):
        z = norm_one(y, m) * gain1 + shift1
        return (z * jax.nn.sigmoid(z) * m).astype(BF16)

    def act_one(i, carry):
        field[1, i] = active(val1[i, 0:C], rmask[i][0:1])
        return carry
    lax.fori_loop(0, PLANES, act_one, 0)
    wait_halo(1)

    def edge_one(d, carry):
        edges[d] = active(halo[0, d, 0:C], near_mask(d))
        return carry
    lax.fori_loop(0, 6, edge_one, 0)

    unfold(1, xb)
    summed = run_conv(w2_ref, xb, store_conv(val2), zero_tile)
    send_halo(2)
    mean2, inv2, per = moments(1, val2, summed)

    def norm_two(y, m):
        return (y - mean2) * m * inv2

    def act_two(i, carry):
        a, b = carry
        m = rmask[i][0:1]
        normed = norm_two(val2[i], m)
        z = normed * gain2 + shift2
        sigma = jax.nn.sigmoid(z)
        tmp[0, i] = z * sigma * m
        gz = cot[i].astype(F32) * (sigma * (1.0 + z * (1.0 - sigma)))
        tmp[1, i] = gz
        return a + gz, b + gz * normed
    sg, gg = lax.fori_loop(0, PLANES, act_two, (zero_tile, zero_tile))

    def send_back(ph, sg, gg):
        send_stats(ph, pack_columns([total(sg), total(gg)]))

    def finish_back(ph, row):
        wait_stats(ph)
        sums = total_stats(ph)
        ng_ref[row:row + 1, :] = sums[1:2, 0:C]
        ng_ref[row + 1:row + 2, :] = sums[0:1, 0:C]
        return to_columns([sums[0:1], sums[1:2]])

    def back(ex, val, gz_slot, near_val, norm, gain, inv, sums):
        sg, gg = sums[0] * per, sums[1] * per
        scaled = gain * inv

        def slope(gz, y, m):
            return (m * scaled * (gz - sg - norm(y, m) * gg)).astype(BF16)

        def body(i, carry):
            g = slope(tmp[gz_slot, i], val[i, 0:C], rmask[i][0:1])
            field[ex, i] = g
            flat[:, pl.ds(pl.multiple_of(i * 128, 128), 128)] = g
            return carry
        lax.fori_loop(0, PLANES, body, 0)
        wait_halo(ex + 1)

        def edge(d, carry):
            edges[d] = slope(halo[ex, d, 0:C], halo[near_val, d, 0:C], near_mask(d))
            return carry
        lax.fori_loop(0, 6, edge, 0)

    send_back(2, sg, gg)
    send_halo(3)
    take(tmp.at[0], out_ref)
    wait_halo(2)
    back(2, val2, 1, 1, norm_two, gain2, inv2, finish_back(2, 2))

    def kernel_grad(w, x):
        for lo, hi in slabs():
            rhs = joined([x[a:b, ox * 128:ox * 128 + PLANES * 128]
                          for ox, a, b in pieces_of(lo, hi)])
            part = lax.dot_general(flat[...], rhs, (((1,), (1,)), ((), ())),
                                   preferred_element_type=F32).astype(BF16)
            for h in range(0, hi - lo, 128):
                tile = part[:, h:min(h + 128, hi - lo)]
                if tile.shape[1] < 128:
                    tile = jnp.concatenate(
                        [tile, jnp.zeros((C, 128 - tile.shape[1]), BF16)], axis=1)
                row = (lo + h) // 128 * C
                grad[w, row:row + C] = tile
        grad[w, 21 * C:GROWS] = jnp.zeros((GROWS - 21 * C, 128), BF16)

    def rows_of(i):
        return pl.ds(pl.multiple_of(i * chunk, chunk), chunk)

    def rs_copy(w, j, peer, slot):
        return pltpu.make_async_remote_copy(
            src_ref=grad.at[w, rows_of(peer)], dst_ref=parts.at[w, slot],
            send_sem=rs_send.at[w, j], recv_sem=rs_recv.at[w, slot],
            device_id=ident(peer), device_id_type=MESH)

    def ag_copy(w, j, peer, slot):
        return pltpu.make_async_remote_copy(
            src_ref=share.at[w], dst_ref=full.at[w, rows_of(slot)],
            send_sem=ag_send.at[w, j], recv_sem=ag_recv.at[w, slot],
            device_id=ident(peer), device_id_type=MESH)

    def start_rs(w):
        parts[w, me] = grad[w, rows_of(me)]
        each_peer(lambda j, peer: rs_copy(w, j, peer, me).start())

    def finish_rs(w):
        each_peer(lambda j, peer: rs_copy(w, j, peer, peer).wait_recv())
        summed = lax.fori_loop(0, group, lambda i, acc: acc + parts[w, i].astype(F32),
                               jnp.zeros((chunk, 128), F32)).astype(BF16)
        share[w] = summed
        full[w, rows_of(me)] = summed
        each_peer(lambda j, peer: ag_copy(w, j, peer, me).start())

    def finish_ag(w, ref):
        each_peer(lambda j, peer: ag_copy(w, j, peer, peer).wait_recv())
        for t in range(21):
            wide = min(128, COLS - t * 128)
            ref[:, t * 128:t * 128 + wide] = full[w, t * C:(t + 1) * C].astype(F32)[:, 0:wide]

    kernel_grad(1, xb)
    start_rs(1)
    unfold(2, xc)

    def store_gz(p, tile, carry):
        a, b = carry
        normed = norm_one(val1[p, 0:C], rmask[p][0:1])
        z = normed * gain1 + shift1
        gz = tile * rmask[p][0:1] * silu_slope(z)
        tmp[2, p] = gz
        return a + gz, b + gz * normed
    sg, gg = run_conv(f2_ref, xc, store_gz, (zero_tile, zero_tile))
    send_back(3, sg, gg)
    send_halo(4)
    finish_rs(1)
    back(3, val1, 2, 0, norm_one, gain1, inv1, finish_back(3, 0))
    kernel_grad(0, xa)
    start_rs(0)
    unfold(3, xc)

    def store_fg(p, tile, carry):
        tmp[0, p] = tile * rmask[p][0:1]
        return carry
    run_conv(f1_ref, xc, store_fg, 0)
    take(tmp.at[0], fg_ref)
    finish_ag(1, wg2_ref)
    finish_rs(0)
    finish_ag(0, wg1_ref)

    for ex in range(5):
        done_halo(ex)
    for ph in range(4):
        done_stats(ph)
    for w in range(2):
        each_peer(lambda j, peer: rs_copy(w, j, peer, me).wait_send())
        each_peer(lambda j, peer: ag_copy(w, j, peer, me).wait_send())


def per_device(nx, ny, feats, voxel_mask, block_slot, block_count, weight_one, weight_two,
               gain_one, shift_one, gain_two, shift_two, cotangent):
    group = nx * ny
    params = jnp.pad(jnp.stack([gain_one, shift_one, gain_two, shift_two]), ((0, 4), (0, 128 - C)))
    vmem = pl.BlockSpec(memory_space=pltpu.VMEM)
    smem = pl.BlockSpec(memory_space=pltpu.SMEM)
    shapes = [
        jax.ShapeDtypeStruct((2, C, 512), BF16),
        jax.ShapeDtypeStruct((2, C, 512), BF16),
        jax.ShapeDtypeStruct((C, COLS), F32),
        jax.ShapeDtypeStruct((C, COLS), F32),
        jax.ShapeDtypeStruct((4, C), F32),
    ]
    wide = (PLANES + 2) * 128
    dma = pltpu.SemaphoreType.DMA
    return pl.pallas_call(
        functools.partial(kernel, nx, ny),
        out_shape=shapes,
        in_specs=[smem, smem] + [vmem] * 2 + [pl.BlockSpec(memory_space=pl.ANY)] * 4,
        out_specs=[vmem] * 5,
        scratch_shapes=[
            pltpu.VMEM((2, C, 512), BF16),
            pltpu.VMEM((2, C, 512), BF16),
            pltpu.VMEM((C, COLS), BF16),
            pltpu.VMEM((C, COLS), BF16),
            dma((4,)),
            pltpu.VMEM((PLANES, 8, 128), F32),
            pltpu.VMEM((4, PLANES, C, 128), BF16),
            pltpu.VMEM((PLANES, C, 128), BF16),
            pltpu.VMEM((PLANES, TALL, 128), F32),
            pltpu.VMEM((PLANES, C, 128), F32),
            pltpu.VMEM((3, PLANES, C, 128), F32),
            pltpu.VMEM((C, PLANES * 128), BF16),
            pltpu.VMEM((9 * C, wide), BF16),
            pltpu.VMEM((9 * C, wide), BF16),
            pltpu.VMEM((9 * C, wide), BF16),
            pltpu.VMEM((21 * 128, 128), F32),
            pltpu.VMEM((C, 21 * 128), BF16),
            pltpu.VMEM((C, 21 * 128), BF16),
            pltpu.VMEM((4, 8, TALL, 128), F32),
            pltpu.VMEM((4, 2, TALL, 128), F32),
            pltpu.VMEM((8, C, 128), BF16),
            pltpu.VMEM((8, C, 128), BF16),
            pltpu.VMEM((2, C, 128), BF16),
            pltpu.VMEM((5, 4, 8, 128), F32),
            pltpu.VMEM((5, 4, 8, 128), F32),
            pltpu.VMEM((4, 8, 128), F32),
            pltpu.VMEM((4, group, 8, 128), F32),
            pltpu.VMEM((2, GROWS, 128), BF16),
            pltpu.VMEM((2, group, GROWS // group, 128), BF16),
            pltpu.VMEM((2, GROWS // group, 128), BF16),
            pltpu.VMEM((2, GROWS, 128), BF16),
            dma((5, 8)), dma((5, 8)),
            dma((4, group)), dma((4, group)),
            dma((2, group)), dma((2, group)),
            dma((2, group)), dma((2, group)),
        ],
        compiler_params=pltpu.CompilerParams(
            collective_id=0, has_side_effects=True, vmem_limit_bytes=60 * 1024 * 1024),
        name="section",
    )(block_slot, block_count, voxel_mask, params, feats, cotangent,
      weight_one, weight_two)


def solution(mesh):
    rows = ("scene", "gx", "gy")
    placed = (
        P(rows, None, None), P(rows, None), P(rows), P(rows),
        P(), P(), P(), P(), P(), P(), P(rows, None, None),
    )
    return jax.shard_map(
        functools.partial(per_device, mesh.shape["gx"], mesh.shape["gy"]),
        mesh=mesh,
        in_specs=placed,
        out_specs=(
            P(rows, None, None), P(rows, None, None),
            P("scene", None), P("scene", None), P("scene", None),
        ),
        check_vma=False,
    )
```
